32 devices in a mesh: seq: 16 (over z, y, x), chan: 2 (over core).
Axes of the slice: x: 2, y: 2, z: 4, core: 2. Of those that a mesh axis runs over, the one named last changes fastest.
Arguments:
- query_rows: bfloat16 [6144, 8192], P('seq', 'chan'), may hold values from -6 to 6
- key_rows: bfloat16 [6144, 8192], P('seq', 'chan'), may hold values from -6 to 6
- value_rows: bfloat16 [6144, 8192], P('seq', 'chan'), may hold values from -6 to 6
- residues: float32 [512, 16], P('chan'), may hold values from -9.2 to 9.2
- decay_rates: float32 [512, 16], P('chan'), may hold values from 7.9752604e-06 to 0.0334
- medium_taps: float32 [512, 128], P('chan'), may hold values from -0.5 to 0.5
- out_gain: float32 [8192], P('chan'), may hold values from 0.1 to 1.9
- reader_plan: int32 [512, 9], P('chan'), may hold values from 0 to 15, as said below
Outputs:
- mixed: bfloat16 [6144, 8192], P('seq', 'chan')
- handoff: float32 [2320, 16, 32], P('seq', None, 'chan')
The draws below stay inside these ranges and needn't reach their ends.
Inputs may be any that keep to these rules, and one draw needn't show every extreme that they name: `reader_plan`: each row names 9 different readers. Within each aligned block of 256 filters (the rows of one device along chan) every reader appears at least once, none more than 145 times, and one reader exactly 145 times.
All inputs are finite; a program needn't handle non-finite values.
Results may differ from the reference program's by a relative error of at most 0.0049.
Values may be sent and summed in bfloat16 or wider, within the bound.
No kernel may reach another device: no remote copies, remote signals or barrier semaphores. Data moves between devices by JAX's collectives and lax.ppermute only.
A program may use at most 128 MiB of HBM per device.

```python
import jax
import jax.numpy as jnp
from jax import lax

D = 8192
GW = 16
MODES = 16
MED = 128
SEQLEN = 6144
FILTERS = 512
GPD = 256
NB = 8
CAP = 145
N_SEQ = 16
N_CHAN = 2


def draw_residues(key, part):
    ramp = jnp.arange(FILTERS).astype(jnp.float32) / max(FILTERS - 1, 1)
    values = jnp.clip(jax.random.normal(key, (FILTERS, MODES), jnp.float32), -4.0, 4.0)
    rising = jnp.exp(jnp.log(3.0) * ramp)
    return 0.6 * values * rising[:, None]


def draw_decay_rates(key, part):
    key_one, key_two, key_three = jax.random.split(key, 3)
    share = 0.5
    slow = jax.random.uniform(key_one, (FILTERS, MODES), jnp.float32) < share
    slow_rate = jnp.exp(jax.random.uniform(key_two, (FILTERS, MODES), jnp.float32, jnp.log(0.05 / SEQLEN), jnp.log(2.0 / SEQLEN)))
    fast_rate = jnp.exp(jax.random.uniform(key_three, (FILTERS, MODES), jnp.float32, jnp.log(1.0 / 50.0), jnp.log(1.0 / 30.0)))
    return jnp.where(slow, slow_rate, fast_rate)


def plan_block(block_key):
    perm_key, shift_key = jax.random.split(block_key, 2)
    order = jax.random.permutation(perm_key, N_SEQ).astype(jnp.int32)
    offset = jax.random.randint(shift_key, (), 0, N_SEQ - 1).astype(jnp.int32)
    hot = order[0]
    others = order[1:]
    rows = jnp.arange(GPD).astype(jnp.int32)[:, None]
    cols = jnp.arange(NB + 1).astype(jnp.int32)[None, :]
    index = rows * (NB + 1) + cols
    is_hot = (rows < CAP) & (cols == 0)
    before = jnp.minimum(rows, CAP) + ((cols > 0) & (rows < CAP)).astype(jnp.int32)
    counter = index - before
    pick = (counter + offset) % (N_SEQ - 1)
    return jnp.where(is_hot, hot, others[pick]).astype(jnp.int32)


def draw_reader_plan(key, part):
    block_keys = jax.random.split(jax.random.fold_in(key, 7), FILTERS // GPD)
    blocks = jax.vmap(plan_block)(block_keys)
    return blocks.reshape(FILTERS, NB + 1)


def levels(rng, dims, pieces, smallest, top_value):
    gain, own = 1.0, jax.random.fold_in(rng, 6)
    for position, parts in pieces:
        heights = jnp.exp(jax.random.uniform(jax.random.fold_in(own, position), (parts,), jnp.float32, smallest / len(pieces), top_value / len(pieces)))
        gain = gain * jnp.repeat(heights, dims[position] // parts).reshape([-1 if axis == position else 1 for axis in range(len(dims))])
    return gain


def centred(rng, extent, spread, reach, cuts=(), kind=jnp.bfloat16):
    gain = levels(rng, extent, cuts, -0.22, 0.18) if cuts else 1.0
    entries = jax.random.normal(rng, extent, jnp.float32) * spread * gain
    return jnp.minimum(jnp.maximum(entries, -reach), reach).astype(kind)


def setup_inputs(seed: int = 0) -> dict:
    keys = jax.random.split(jax.random.key(seed), 9)
    query_rows = centred(keys[0], (SEQLEN, D), 1.0, 6.0, ((0, 16), (1, 2)))
    key_rows = centred(keys[1], (SEQLEN, D), 1.0, 6.0, ((0, 16), (1, 2)))
    value_rows = centred(keys[2], (SEQLEN, D), 1.0, 6.0, ((0, 16), (1, 2)))
    residues = draw_residues(jax.random.fold_in(keys[8], 71), 0)
    decay_rates = draw_decay_rates(jax.random.fold_in(keys[8], 71), 0)
    medium_taps = centred(keys[5], (FILTERS, MED), MED ** -0.5, 0.5, ((0, 2),), jnp.float32)
    out_gain = jnp.clip(1.0 + 0.18 * jax.random.normal(keys[6], (D,), jnp.float32), 0.1, 1.9)
    reader_plan = draw_reader_plan(jax.random.fold_in(keys[8], 71), 0)
    return dict(query_rows=query_rows, key_rows=key_rows, value_rows=value_rows, residues=residues, decay_rates=decay_rates, medium_taps=medium_taps, out_gain=out_gain, reader_plan=reader_plan)


def reference(query_rows, key_rows, value_rows, residues, decay_rates, medium_taps, out_gain, reader_plan):
    highest = lax.Precision.HIGHEST
    product = (key_rows.astype(jnp.float32) * value_rows.astype(jnp.float32)).astype(jnp.bfloat16)
    norm_factor = jnp.sqrt(-jnp.expm1(-2.0 * decay_rates))
    positions = jnp.arange(SEQLEN).astype(jnp.float32)
    grouped = product.reshape(SEQLEN, FILTERS, GW).transpose(1, 0, 2)
    queries = query_rows.reshape(SEQLEN, FILTERS, GW).transpose(1, 0, 2)

    def per_filter(operands):
        rows, query_part, coeffs, rates, taps, factor = operands
        rows = rows.astype(jnp.float32)
        decays = jnp.exp(-rates[:, None] * positions[None, :])
        response = jnp.dot(coeffs * factor, decays, precision=highest) + jnp.pad(taps, (0, SEQLEN - MED))
        length = 2 * SEQLEN
        spectrum = jnp.fft.rfft(response, length)[:, None] * jnp.fft.rfft(rows, length, axis=0)
        conv = jnp.fft.irfft(spectrum, length, axis=0)[:SEQLEN].astype(jnp.float32)
        gated = query_part.astype(jnp.float32) * conv
        ends = jnp.exp(-rates[:, None] * (SEQLEN - positions)[None, :])
        state = factor[:, None] * jnp.dot(ends, rows, precision=highest)
        tail = rows[SEQLEN - MED:].reshape(NB, MODES, GW)
        items = jnp.concatenate([tail, state[None]], axis=0)
        return (gated, items)
    gated, items = lax.map(per_filter, (grouped, queries, residues, decay_rates, medium_taps, norm_factor))
    energy = lax.optimization_barrier(jnp.sum(lax.optimization_barrier(jnp.sum(gated * gated, axis=2)), axis=0))
    scale = lax.rsqrt(energy / D + 1e-05)
    gated = gated.transpose(1, 0, 2).reshape(SEQLEN, D)
    mixed = (gated * scale[:, None] * out_gain[None, :]).astype(jnp.bfloat16)
    flat_items = items.reshape(N_CHAN, GPD * (NB + 1), MODES * GW)
    plan_blocks = reader_plan.reshape(N_CHAN, GPD * (NB + 1))
    readers = jnp.arange(N_SEQ).astype(jnp.int32)
    chosen = plan_blocks[:, None, :] == readers[None, :, None]
    ranks = jnp.cumsum(chosen.astype(jnp.int32), axis=2) - 1
    slots = jnp.arange(CAP).astype(jnp.int32)
    select = (chosen[:, :, None, :] & (ranks[:, :, None, :] == slots[None, None, :, None])).astype(jnp.float32)
    handoff = jnp.einsum('nrji,nip->nrjp', select, flat_items.astype(jnp.float32), precision=highest)
    handoff = handoff.reshape(N_CHAN, N_SEQ * CAP, MODES, GW).transpose(1, 2, 0, 3).reshape(N_SEQ * CAP, MODES, N_CHAN * GW)
    return (mixed, handoff)
```

```python
import functools
import math

import jax
import jax.numpy as jnp
from jax import lax
from jax.experimental import pallas as pl
from jax.experimental.pallas import tpu as pltpu
from jax.sharding import PartitionSpec as P

D = 8192
GW = 16
MODES = 16
CH = 128
LANES = 128
PER_TILE = LANES // GW
f32 = jnp.float32
bf16 = jnp.bfloat16
highest = lax.Precision.HIGHEST


def params(mib=56):
    return pltpu.CompilerParams(vmem_limit_bytes=mib * 1024 * 1024)


def iota(shape, axis):
    return lax.broadcasted_iota(jnp.int32, shape, axis)


def same_filter(rows, lanes):
    return (iota((rows, lanes), 0) // MODES) == ((iota((rows, lanes), 1) % LANES) // GW)


def tn_dot(a, b, precision=None):
    return lax.dot_general(
        a, b, (((0,), (0,)), ((), ())), preferred_element_type=f32, precision=precision
    )


def by_tile(values):
    groups = values.shape[0]
    copies = (iota((MODES, LANES), 1) % MODES == iota((MODES, LANES), 0)).astype(f32)
    wide = jnp.dot(values, copies, preferred_element_type=f32, precision=highest)
    mine = (iota((groups, LANES), 1) // MODES) == (iota((groups, LANES), 0) % PER_TILE)
    return jnp.where(mine, wide, 0.0).reshape(groups // PER_TILE, PER_TILE, LANES).sum(axis=1)


def product_kernel(
    tiles, k_ref, v_ref, rates_ref, x_ref, tail_ref, p1_ref, p2_ref, own_ref, sent_ref, spread_ref, rows_ref, flat_ref
):
    step = pl.program_id(0)

    @pl.when(step == 0)
    def _():
        rates = rates_ref[...].T
        flat_ref[...] = rates
        rows_ref[...] = by_tile(rates)

    to_end = (CH - iota((CH, LANES), 0)).astype(f32)
    mask = same_filter(LANES, 3 * LANES)
    expand = (iota((PER_TILE, LANES), 1) // GW == iota((PER_TILE, LANES), 0)).astype(f32)
    for t in range(tiles):
        lanes = slice(t * LANES, (t + 1) * LANES)
        tile = step * tiles + t
        x = (k_ref[:, lanes].astype(f32) * v_ref[:, lanes].astype(f32)).astype(bf16)
        x_ref[:, lanes] = x
        tail_ref[:, lanes] = x[2 * CH :]
        spread = tn_dot(flat_ref[pl.ds(pl.multiple_of(tile * PER_TILE, PER_TILE), PER_TILE), :], expand, highest)
        spread_ref[:, lanes] = spread
        ends = jnp.exp(-to_end * rows_ref[pl.ds(tile, 1), :]).astype(bf16)
        wide = jnp.concatenate([x[:CH], x[CH : 2 * CH], x[2 * CH :]], axis=1)
        full = tn_dot(ends, wide)
        packed = jnp.where(mask, full, 0.0).reshape(PER_TILE, MODES, 3 * LANES).sum(axis=0)
        u0, u1, u2 = packed[:, :LANES], packed[:, LANES : 2 * LANES], packed[:, 2 * LANES :]
        decay = jnp.exp(-float(CH) * spread)
        p2 = decay * u0 + u1
        own = decay * p2 + u2
        p1_ref[:, lanes] = u0
        p2_ref[:, lanes] = p2
        own_ref[:, lanes] = own
        sent_ref[:, lanes] = own.astype(bf16)


def product_and_states(key_rows, value_rows, rates_t):
    tokens, channels = key_rows.shape
    groups = rates_t.shape[1]
    tiles = 8
    width = tiles * LANES
    wide = pl.BlockSpec((tokens, width), lambda i: (0, i))
    state = pl.BlockSpec((MODES, width), lambda i: (0, i))
    state_shape = jax.ShapeDtypeStruct((MODES, channels), f32)
    whole = lambda *shape: pl.BlockSpec(shape, lambda i: (0, 0))
    return pl.pallas_call(
        functools.partial(product_kernel, tiles),
        grid=(channels // width,),
        in_specs=[wide, wide, whole(*rates_t.shape)],
        out_specs=[
            wide, pl.BlockSpec((CH, width), lambda i: (0, i)), state, state, state, state, state,
            whole(channels // LANES, LANES),
        ],
        out_shape=[
            jax.ShapeDtypeStruct((tokens, channels), bf16), jax.ShapeDtypeStruct((CH, channels), bf16),
            state_shape, state_shape, state_shape, jax.ShapeDtypeStruct((MODES, channels), bf16), state_shape,
            jax.ShapeDtypeStruct((channels // LANES, LANES), f32),
        ],
        scratch_shapes=[pltpu.VMEM((groups, MODES), f32)],
        compiler_params=params(),
        cost_estimate=pl.CostEstimate(
            flops=6 * tokens * channels * CH, bytes_accessed=6 * tokens * channels, transcendentals=channels * CH
        ),
        name="product_states",
    )(key_rows, value_rows, rates_t)


FOLD = 4
PARTS = PER_TILE // FOLD


def toeplitz(row):
    return pltpu.roll(jnp.broadcast_to(row, (CH, LANES)), 0, 1, stride=1, stride_axis=0)


def fold_masks():
    group = iota((CH, LANES), 1) // GW
    return [(group % PARTS == a).astype(f32).astype(bf16) for a in range(PARTS)]


def unfold(stacked):
    member = iota((CH, LANES), 1) // GW // PARTS
    out = stacked[:CH]
    for b in range(1, FOLD):
        out = jnp.where(member == b, stacked[b * CH : (b + 1) * CH], out)
    return out


def reversed_lags(taps):
    flip = ((iota((CH, LANES), 0) + iota((CH, LANES), 1)) % CH == 0).astype(f32)
    return jnp.dot(taps, flip, preferred_element_type=f32, precision=highest)


def local_kernel(first, tiles, x_ref, taps_ref, rates_ref, coeff_ref, *rest):
    out_ref, taps_rev, response, lhs_all, rhs_all = rest[-5:]
    step = pl.program_id(0)
    count = tiles * PER_TILE
    half = PARTS * CH
    at = pl.multiple_of(step * count, count)
    lag = ((CH - iota((1, LANES), 1)) % CH).astype(f32)

    @pl.when(step == 0)
    def _():
        span = slice(first, first + taps_ref.shape[0])
        rates, coeff = rates_ref[...].T[span], coeff_ref[...].T[span]
        sums = reversed_lags(taps_ref[...])
        taps_rev[...] = sums
        for m in range(MODES):
            sums = sums + coeff[:, m : m + 1] * jnp.exp(-rates[:, m : m + 1] * lag)
        response[...] = sums

    lower = iota((CH, LANES), 1) <= iota((CH, LANES), 0)
    masks = fold_masks()
    for t in range(tiles):
        lanes = slice(t * LANES, (t + 1) * LANES)
        lhs_ref, rhs_ref = lhs_all.at[t % 2], rhs_all.at[t % 2]
        chunks = [x_ref[c * CH : (c + 1) * CH, lanes] for c in range(3)]
        for f in range(PER_TILE):
            a, rows = f % PARTS, slice(f // PARTS * CH, (f // PARTS + 1) * CH)
            row = pl.ds(at + t * PER_TILE + f, 1)
            lhs_ref[rows, half + a * CH : half + (a + 1) * CH] = jnp.where(lower, toeplitz(response[row, :]), 0.0).astype(bf16)
            lhs_ref[rows, a * CH : (a + 1) * CH] = jnp.where(lower, 0.0, toeplitz(taps_rev[row, :])).astype(bf16)
        for a in range(PARTS):
            x0, x1, x2 = [chunk * masks[a] for chunk in chunks]
            rhs_ref[a * CH : (a + 1) * CH, :LANES] = x0
            rhs_ref[a * CH : (a + 1) * CH, LANES:] = x1
            rhs_ref[half + a * CH : half + (a + 1) * CH, :LANES] = x1
            rhs_ref[half + a * CH : half + (a + 1) * CH, LANES:] = x2
        later = jnp.dot(lhs_ref[...], rhs_ref[...], preferred_element_type=f32)
        first = jnp.dot(lhs_ref[:, half:], rhs_ref[:half, :LANES], preferred_element_type=f32)
        out_ref[:CH, lanes] = unfold(first)
        out_ref[CH : 2 * CH, lanes] = unfold(later[:, :LANES])
        out_ref[2 * CH :, lanes] = unfold(later[:, LANES:])


def local_part(x, taps, rates_t, coeff_t, piece, pieces, into):
    tokens, channels = x.shape
    groups = taps.shape[0]
    tiles = min(4, channels // LANES // pieces)
    width = tiles * LANES
    steps = channels // width // pieces
    start = piece * steps
    span = groups // pieces
    wide = pl.BlockSpec((tokens, width), lambda i: (0, i + start))
    whole = pl.BlockSpec(rates_t.shape, lambda i: (0, 0))
    args = [x, taps, rates_t, coeff_t]
    specs = [
        wide, pl.BlockSpec((span, CH), lambda i: (piece, 0)), whole, whole,
    ]
    aliases = {}
    if into is not None:
        args.append(into)
        specs.append(pl.BlockSpec(memory_space=pl.ANY))
        aliases = {4: 0}
    return pl.pallas_call(
        functools.partial(local_kernel, piece * span, tiles),
        grid=(steps,),
        in_specs=specs,
        out_specs=wide,
        out_shape=jax.ShapeDtypeStruct((tokens, channels), f32),
        scratch_shapes=[
            pltpu.VMEM((span, CH), f32), pltpu.VMEM((span, CH), f32),
            pltpu.VMEM((2, FOLD * CH, 2 * PARTS * CH), bf16), pltpu.VMEM((2, 2 * PARTS * CH, 2 * LANES), bf16),
        ],
        input_output_aliases=aliases,
        compiler_params=params(),
        cost_estimate=pl.CostEstimate(
            flops=span * CH * 256 * 512 * 2, bytes_accessed=span * GW * tokens * 6, transcendentals=0
        ),
        name="local_conv",
    )(*args)


def cross_of(decays, states):
    mask = same_filter(LANES, len(states) * LANES)
    wide = jnp.concatenate(states, axis=1)
    high = wide.astype(bf16)
    low = wide - high.astype(f32)
    blocks = lambda a: jnp.where(mask, jnp.concatenate([a] * PER_TILE, axis=0), 0.0).astype(bf16)
    stacked = jnp.concatenate([blocks(high.astype(f32)), blocks(low)], axis=0)
    return jnp.dot(jnp.concatenate([decays, decays], axis=1), stacked, preferred_element_type=f32)


def starts_of(lam, weight):
    index = iota((CH, LANES), 0).astype(f32)
    return (weight * jnp.exp(-index * lam)).astype(bf16)


def add_energy(energy_ref, total_ref, step, last, partial):
    @pl.when(step == 0)
    def _():
        total_ref[...] = partial

    @pl.when(step > 0)
    def _():
        total_ref[...] += partial

    @pl.when(step == last)
    def _():
        energy_ref[...] = lax.dot_general(
            jnp.ones((8, LANES), f32), total_ref[...], (((1,), (1,)), ((), ())),
            preferred_element_type=f32, precision=highest,
        )


def later_kernel(
    tiles, steps, local1_ref, local2_ref, q1_ref, q2_ref, in_ref, p1_ref, p2_ref, spread_ref, rates_ref, coeff_ref,
    gated_ref, energy_ref, total_ref, weight_ref,
):
    step = pl.program_id(0)

    @pl.when(step == 0)
    def _():
        weight_ref[...] = by_tile(coeff_ref[...].T)

    partial = jnp.zeros((2 * CH, LANES), f32)
    for t in range(tiles):
        lanes = slice(t * LANES, (t + 1) * LANES)
        decay = jnp.exp(-float(CH) * spread_ref[:, lanes])
        entry = decay * in_ref[:, lanes]
        z1 = entry + p1_ref[:, lanes]
        z2 = decay * entry + p2_ref[:, lanes]
        row = pl.ds(step * tiles + t, 1)
        cross = cross_of(starts_of(rates_ref[row, :], weight_ref[row, :]), [z1, z2])
        one = (local1_ref[:, lanes] + cross[:, :LANES]) * q1_ref[:, lanes].astype(f32)
        two = (local2_ref[:, lanes] + cross[:, LANES:]) * q2_ref[:, lanes].astype(f32)
        gated_ref[:CH, lanes] = one
        gated_ref[CH:, lanes] = two
        partial = partial + jnp.concatenate([one * one, two * two], axis=0)
    add_energy(energy_ref, total_ref, step, steps - 1, partial)


def first_kernel(
    tiles, steps, local_ref, q_ref, in_ref, tail_ref, taps_ref, rates_ref, coeff_ref,
    gated_ref, energy_ref, total_ref, weight_ref, taps_rev, lhs_all,
):
    step = pl.program_id(0)

    @pl.when(step == 0)
    def _():
        weight_ref[...] = by_tile(coeff_ref[...].T)

    taps_rev[...] = reversed_lags(taps_ref[...])
    lower = iota((CH, LANES), 1) <= iota((CH, LANES), 0)
    masks = fold_masks()
    partial = jnp.zeros((CH, LANES), f32)
    for t in range(tiles):
        lanes = slice(t * LANES, (t + 1) * LANES)
        lhs_ref = lhs_all.at[t % 2]
        row = pl.ds(step * tiles + t, 1)
        cross = cross_of(starts_of(rates_ref[row, :], weight_ref[row, :]), [in_ref[:, lanes]])
        for f in range(PER_TILE):
            a, rows = f % PARTS, slice(f // PARTS * CH, (f // PARTS + 1) * CH)
            at = t * PER_TILE + f
            lhs_ref[rows, a * CH : (a + 1) * CH] = jnp.where(lower, 0.0, toeplitz(taps_rev[at : at + 1, :])).astype(bf16)
        tail = tail_ref[:, lanes]
        masked = jnp.concatenate([tail * mask for mask in masks], axis=0)
        carried = unfold(jnp.dot(lhs_ref[...], masked, preferred_element_type=f32))
        one = (local_ref[:, lanes] + cross + carried) * q_ref[:, lanes].astype(f32)
        gated_ref[:, lanes] = one
        partial = partial + one * one
    add_energy(energy_ref, total_ref, step, steps - 1, partial)


def later_part(local, query_rows, incoming, p1, p2, rates_spread, rate_rows, coeff_t):
    tokens, channels = local.shape
    tiles = 8
    width = tiles * LANES
    steps = channels // width
    state = pl.BlockSpec((MODES, width), lambda i: (0, i))
    whole = lambda a: pl.BlockSpec(a.shape, lambda i: (0, 0))
    chunk = lambda c: pl.BlockSpec((CH, width), lambda i: (c, i))
    return pl.pallas_call(
        functools.partial(later_kernel, tiles, steps),
        grid=(steps,),
        in_specs=[
            chunk(1), chunk(2), chunk(1), chunk(2),
            state, state, state, state, whole(rate_rows), whole(coeff_t),
        ],
        out_specs=[
            pl.BlockSpec((2 * CH, width), lambda i: (0, i)),
            pl.BlockSpec((8, 2 * CH), lambda i: (0, 0)),
        ],
        out_shape=[
            jax.ShapeDtypeStruct((2 * CH, channels), f32),
            jax.ShapeDtypeStruct((8, 2 * CH), f32),
        ],
        scratch_shapes=[pltpu.VMEM((2 * CH, LANES), f32), pltpu.VMEM(rate_rows.shape, f32)],
        compiler_params=params(),
        cost_estimate=pl.CostEstimate(
            flops=channels // LANES * CH * 256 * 512, bytes_accessed=channels * 2 * CH * 10, transcendentals=channels * CH
        ),
        name="gate_later",
    )(local, local, query_rows, query_rows, incoming, p1, p2, rates_spread, rate_rows, coeff_t)


def first_part(local, query_rows, incoming, tail, taps, rate_rows, coeff_t):
    tokens, channels = local.shape
    tiles = 8
    width = tiles * LANES
    steps = channels // width
    top = pl.BlockSpec((CH, width), lambda i: (0, i))
    whole = lambda a: pl.BlockSpec(a.shape, lambda i: (0, 0))
    return pl.pallas_call(
        functools.partial(first_kernel, tiles, steps),
        grid=(steps,),
        in_specs=[
            top, top, pl.BlockSpec((MODES, width), lambda i: (0, i)), top,
            pl.BlockSpec((tiles * PER_TILE, CH), lambda i: (i, 0)), whole(rate_rows), whole(coeff_t),
        ],
        out_specs=[top, pl.BlockSpec((8, CH), lambda i: (0, 0))],
        out_shape=[jax.ShapeDtypeStruct((CH, channels), f32), jax.ShapeDtypeStruct((8, CH), f32)],
        scratch_shapes=[
            pltpu.VMEM((CH, LANES), f32), pltpu.VMEM(rate_rows.shape, f32),
            pltpu.VMEM((tiles * PER_TILE, CH), f32), pltpu.VMEM((2, FOLD * CH, PARTS * CH), bf16),
        ],
        compiler_params=params(),
        cost_estimate=pl.CostEstimate(
            flops=channels * CH * 1024, bytes_accessed=channels * CH * 12, transcendentals=channels * CH
        ),
        name="gate_first",
    )(local, query_rows, incoming, tail, taps, rate_rows, coeff_t)


def norm_kernel(energy_ref, gated_ref, gain_ref, *rest):
    out_ref = rest[-1]
    spread = tn_dot(energy_ref[...], jnp.full((8, LANES), 0.125, f32), highest)
    scale = lax.rsqrt(spread / D + 1e-05)
    for t in range(out_ref.shape[1] // LANES):
        lanes = slice(t * LANES, (t + 1) * LANES)
        out_ref[:, lanes] = (gated_ref[:, lanes] * scale * gain_ref[:, lanes]).astype(bf16)


def norm_part(energy, gated, gain_row, tokens, first, into):
    rows, channels = gated.shape
    width = min(channels, 16 * LANES)
    per = CH
    args = [energy, gated, gain_row]
    specs = [
        pl.BlockSpec((8, per), lambda r, i: (0, r)),
        pl.BlockSpec((per, width), lambda r, i: (r, i)),
        pl.BlockSpec((1, width), lambda r, i: (0, i)),
    ]
    aliases = {}
    if into is not None:
        args.append(into)
        specs.append(pl.BlockSpec(memory_space=pl.ANY))
        aliases = {3: 0}
    return pl.pallas_call(
        norm_kernel,
        grid=(rows // per, channels // width),
        in_specs=specs,
        out_specs=pl.BlockSpec((per, width), lambda r, i: (r + first // per, i)),
        out_shape=jax.ShapeDtypeStruct((tokens, channels), bf16),
        input_output_aliases=aliases,
        compiler_params=params(),
        cost_estimate=pl.CostEstimate(flops=rows * channels * 2, bytes_accessed=rows * channels * 6, transcendentals=0),
        name="norm",
    )(*args)


def regroup(block):
    shape = block.shape
    sub = iota(shape, 1)
    lane = iota(shape, 2) // GW
    for k in (1, 2, 4):
        up = pltpu.roll(pltpu.roll(block, 8 - k, 1), GW * k, 2)
        down = pltpu.roll(pltpu.roll(block, k, 1), LANES - GW * k, 2)
        row_bit, lane_bit = (sub & k) != 0, (lane & k) != 0
        block = jnp.where(row_bit == lane_bit, block, jnp.where(lane_bit, up, down))
    return block


def ranks_of(present):
    count = present.shape[1]
    before = (iota((count, count), 0) < iota((count, count), 1)).astype(bf16)
    return jnp.dot(present.astype(bf16), before, preferred_element_type=f32)


def select_kernel(blocks, slots, inner, outer, me_ref, tail_ref, plan_ref, *refs):
    outs, (items_ref, picks_ref) = refs[:inner], refs[inner:]
    groups = plan_ref.shape[1]

    @pl.when(me_ref[0] != inner * outer - 1)
    def _():
        for out in outs:
            out[...] = jnp.zeros_like(out)

    @pl.when(me_ref[0] == inner * outer - 1)
    def _():
        for g in range(0, groups // PER_TILE, 2):
            halves = []
            for side in range(2):
                rows = tail_ref[:, (g + side) * LANES : (g + side + 1) * LANES].astype(f32)
                halves.append(regroup(rows.reshape(2 * blocks, 8, LANES)))
            for b in range(blocks):
                for half in range(2):
                    both = jnp.concatenate([halves[0][2 * b + half], halves[1][2 * b + half]], axis=0)
                    items_ref[
                        b * groups + g * 8 : b * groups + (g + 2) * 8, half * LANES : (half + 1) * LANES
                    ] = both.astype(bf16)
        plan = plan_ref[...]
        readers = iota((inner * outer, 1, 1), 0)
        mine = (plan[None] == readers).astype(f32)
        ranks = ranks_of(jnp.sum(mine, axis=1))
        slot = iota((slots, groups), 0).astype(f32)
        for p in range(inner):
            for o in range(outer):
                r = o * inner + p
                at = jnp.broadcast_to(ranks[r : r + 1], (slots, groups)) == slot
                for b in range(blocks):
                    picks_ref[o * slots : (o + 1) * slots, b * groups : (b + 1) * groups] = jnp.where(
                        at & (plan[b : b + 1] == r), 1.0, 0.0
                    ).astype(bf16)
            total = jnp.dot(picks_ref[...], items_ref[...], preferred_element_type=f32)
            outs[p][...] = total.astype(bf16).reshape(outs[p].shape)


def select_tails(me, tail, plan_cols, inner, outer, slots):
    rows, channels = tail.shape
    groups = plan_cols.shape[1]
    blocks = rows // MODES
    vmem = pl.BlockSpec(memory_space=pltpu.VMEM)
    return pl.pallas_call(
        functools.partial(select_kernel, blocks, slots, inner, outer),
        in_specs=[pl.BlockSpec(memory_space=pltpu.SMEM), vmem, vmem],
        out_specs=[vmem] * inner,
        out_shape=[jax.ShapeDtypeStruct((outer, slots, MODES * GW), bf16)] * inner,
        scratch_shapes=[
            pltpu.VMEM((blocks * groups, MODES * GW), bf16), pltpu.VMEM((outer * slots, blocks * groups), bf16),
        ],
        compiler_params=params(),
        cost_estimate=pl.CostEstimate(flops=10**9, bytes_accessed=2 * 10**6, transcendentals=0),
        name="select_tails",
    )(me, tail, plan_cols)


def handoff_kernel(me_ref, final_ref, norm_ref, plan_ref, got_ref, out_ref, items_ref):
    groups = plan_ref.shape[1]
    capacity = out_ref.shape[2]
    slots = got_ref.shape[0]
    plan = plan_ref[...]
    mine = plan == me_ref[0]
    present = jnp.sum(mine.astype(f32), axis=0, keepdims=True)
    rank = ranks_of(jnp.broadcast_to(present, (8, groups)))[:1]
    final = final_ref[...] * norm_ref[...]
    stack = [
        final[half * 8 : (half + 1) * 8, g * LANES : (g + 1) * LANES]
        for half in range(2) for g in range(groups // PER_TILE)
    ]
    done = regroup(jnp.stack(stack, axis=0)).reshape(2 * groups, LANES).astype(bf16)
    items_ref[:, :LANES] = done[:groups]
    items_ref[:, LANES:] = done[groups:]
    slot = iota((slots, groups), 0).astype(f32)
    last = plan.shape[0] - 1
    at = (jnp.broadcast_to(rank, (slots, groups)) == slot) & mine[last:]
    pick = jnp.where(at, 1.0, 0.0).astype(bf16)
    rows = jnp.dot(pick, items_ref[...], preferred_element_type=f32)
    rows = (rows + got_ref[...].astype(f32)).T
    out_ref[...] = rows[:, :capacity].reshape(out_ref.shape)


def assemble(me, final, norm_spread, plan_cols, got, capacity):
    groups = plan_cols.shape[1]
    vmem = pl.BlockSpec(memory_space=pltpu.VMEM)
    out = pl.pallas_call(
        handoff_kernel,
        in_specs=[pl.BlockSpec(memory_space=pltpu.SMEM), vmem, vmem, vmem, vmem],
        out_specs=vmem,
        out_shape=jax.ShapeDtypeStruct((MODES, GW, capacity), f32),
        scratch_shapes=[pltpu.VMEM((groups, MODES * GW), bf16)],
        compiler_params=params(),
        cost_estimate=pl.CostEstimate(flops=10**9, bytes_accessed=10**6, transcendentals=0),
        name="handoff",
    )(me, final, norm_spread, plan_cols, got)
    return out.transpose(2, 0, 1)


def scatter_tails(selected, inner, outer):
    count = inner * outer
    me = lax.axis_index("seq")
    base = count - inner
    mine = selected[inner - 1]
    for p in range(inner - 1):
        sent = lax.ppermute(selected[p], "seq", [(count - 1, base + p)])
        mine = jnp.where(me == base + p, sent, mine)
    got = mine[outer - 1]
    for o in range(outer - 1):
        sent = lax.ppermute(mine[o], "seq", [(base + p, o * inner + p) for p in range(inner)])
        got = jnp.where(me // inner == o, sent, got)
    return got


def scan_states(own, sent, rates_spread, tokens):
    count = lax.axis_size("seq")
    me = lax.axis_index("seq")
    total, incoming = own, jnp.zeros_like(own)
    step = 1
    while step < count:
        pairs = [(i, i ^ step) for i in range(count)]
        other = lax.ppermute(sent, "seq", pairs).astype(f32)
        right = (me & step) != 0
        offset = ((me & (step - 1)) * tokens).astype(f32)
        incoming = jnp.where(right, incoming + jnp.exp(-rates_spread * offset) * other, incoming)
        decay = jnp.exp(-rates_spread * float(step * tokens))
        total = jnp.where(right, decay * other + total, decay * total + other)
        sent = total.astype(bf16)
        step *= 2
    return total, incoming


def sum_over_chan(energy):
    if lax.axis_size("chan") == 2:
        return energy + lax.ppermute(energy, "chan", [(0, 1), (1, 0)])
    return lax.psum(energy, "chan")


def per_device(
    query_rows, key_rows, value_rows, residues, decay_rates, medium_taps, out_gain, reader_plan
):
    tokens, channels = query_rows.shape
    groups, mode_count = residues.shape
    blocks = medium_taps.shape[1] // mode_count
    seq_count = lax.axis_size("seq")
    me = lax.axis_index("seq")

    rates_t = decay_rates.T
    x, own_tail, p1, p2, own, sent, rates_spread, rate_rows = product_and_states(
        key_rows, value_rows, rates_t
    )
    tail_prev = lax.ppermute(own_tail, "seq", [(i, i + 1) for i in range(seq_count - 1)])
    total, incoming = scan_states(own, sent, rates_spread, tokens)

    coeff_t = residues.T * jnp.sqrt(-jnp.expm1(-2.0 * rates_t))
    norm_spread = jnp.sqrt(-jnp.expm1(-2.0 * rates_spread))
    plan_cols = reader_plan.T

    inner = 1 << (int(math.log2(seq_count)) // 2)
    outer = seq_count // inner
    capacity = (groups * (blocks + 1) + seq_count - 1) // seq_count + 1
    slots = -(-capacity // 16) * 16
    selected = select_tails(me.reshape(1), own_tail, plan_cols, inner, outer, slots)
    got = scatter_tails(selected, inner, outer)

    pieces = 4
    local = None
    for piece in range(pieces):
        local = local_part(x, medium_taps, rates_t, coeff_t, piece, pieces, local)

    gain_row = out_gain[None, :]
    gated_later, energy_later = later_part(
        local, query_rows, incoming, p1, p2, rates_spread, rate_rows, coeff_t
    )
    mixed = norm_part(sum_over_chan(energy_later), gated_later, gain_row, tokens, CH, None)
    gated_first, energy_first = first_part(
        local, query_rows, incoming, tail_prev, medium_taps, rate_rows, coeff_t
    )
    mixed = norm_part(sum_over_chan(energy_first), gated_first, gain_row, tokens, 0, mixed)

    handoff = assemble(me.reshape(1), total, norm_spread, plan_cols, got, capacity)
    return mixed, handoff


def solution(mesh):
    placed = (
        P("seq", "chan"),
        P("seq", "chan"),
        P("seq", "chan"),
        P("chan", None),
        P("chan", None),
        P("chan", None),
        P("chan"),
        P("chan", None),
    )
    return jax.shard_map(
        per_device,
        mesh=mesh,
        in_specs=placed,
        out_specs=(P("seq", "chan"), P("seq", None, "chan")),
        check_vma=False,
    )
```

```python
import functools
import math

import jax
import jax.numpy as jnp
from jax import lax
from jax.experimental import pallas as pl
from jax.experimental.pallas import tpu as pltpu
from jax.sharding import PartitionSpec as P

D = 8192
GW = 16
MODES = 16
CH = 128
LANES = 128
PER_TILE = LANES // GW
f32 = jnp.float32
bf16 = jnp.bfloat16
highest = lax.Precision.HIGHEST


def params(mib=20):
    return pltpu.CompilerParams(vmem_limit_bytes=mib * 1024 * 1024)


def iota(shape, axis):
    return lax.broadcasted_iota(jnp.int32, shape, axis)


def same_filter(rows, lanes):
    return (iota((rows, lanes), 0) // MODES) == ((iota((rows, lanes), 1) % LANES) // GW)


def tn_dot(a, b, precision=None):
    return lax.dot_general(
        a, b, (((0,), (0,)), ((), ())), preferred_element_type=f32, precision=precision
    )


def by_tile(values):
    groups = values.shape[0]
    copies = (iota((MODES, LANES), 1) % MODES == iota((MODES, LANES), 0)).astype(f32)
    wide = jnp.dot(values, copies, preferred_element_type=f32, precision=highest)
    mine = (iota((groups, LANES), 1) // MODES) == (iota((groups, LANES), 0) % PER_TILE)
    return jnp.where(mine, wide, 0.0).reshape(groups // PER_TILE, PER_TILE, LANES).sum(axis=1)


ANY = pl.BlockSpec(memory_space=pl.ANY)
VMEM = pl.BlockSpec(memory_space=pltpu.VMEM)
HBM = pl.BlockSpec(memory_space=pltpu.HBM)


def lanes_at(index, width):
    return pl.ds(pl.multiple_of(index * width, width), width)


def copies(pairs, sems, chunk, width):
    out = []
    for i, (source, target, from_lane, to_lane) in enumerate(pairs):
        out.append(
            pltpu.make_async_copy(
                source.at[:, pl.ds(pl.multiple_of(from_lane + chunk * width, LANES), width)],
                target.at[:, pl.ds(pl.multiple_of(to_lane + chunk * width, LANES), width)],
                sems.at[i, chunk],
            )
        )
    return out


def drain(chunks, width, outputs, out_sems):
    for c in range(chunks):
        for copy in copies(outputs, out_sems, c, width):
            copy.wait()


def product_of(k_ref, v_ref, lanes):
    return (k_ref[:, lanes].astype(f32) * v_ref[:, lanes].astype(f32)).astype(bf16)


def product_kernel(
    chunks, tiles, k_hbm, v_hbm, rates_ref, tail_ref, p1_ref, p2_ref, own_ref, sent_ref, rows_ref,
    k_ref, v_ref, in_sems,
):
    width = tiles * LANES
    inputs = [(k_hbm, k_ref, 0, 0), (v_hbm, v_ref, 0, 0)]
    for c in range(chunks):
        for copy in copies(inputs, in_sems, c, width):
            copy.start()
    rows_ref[...] = by_tile(rates_ref[...].T)
    to_end = (CH - iota((CH, LANES), 0)).astype(f32)
    mask = same_filter(LANES, 3 * LANES)
    none = jnp.zeros((CH, LANES), bf16)

    @pl.loop(0, chunks)
    def _(c):
        for copy in copies(inputs, in_sems, c, width):
            copy.wait()
        for t in range(tiles):
            lanes = lanes_at(c * tiles + t, LANES)
            x = product_of(k_ref, v_ref, lanes)
            tail_ref[:, lanes] = x[2 * CH :]
            lam = rows_ref[pl.ds(c * tiles + t, 1), :]
            near = jnp.exp(-to_end * lam)
            decay = jnp.exp(-float(CH) * lam)
            middle = near * decay
            ends = jnp.concatenate([(middle * decay).astype(bf16), middle.astype(bf16), near.astype(bf16)], axis=0)
            x0, x1 = x[:CH], x[CH : 2 * CH]
            wide = jnp.concatenate(
                [x, jnp.concatenate([none, x0, x1], axis=0), jnp.concatenate([none, none, x0], axis=0)], axis=1
            )
            full = tn_dot(ends, wide)
            packed = jnp.where(mask, full, 0.0).reshape(PER_TILE, MODES, 3 * LANES).sum(axis=0)
            own_ref[:, lanes] = packed[:, :LANES]
            sent_ref[:, lanes] = packed[:, :LANES].astype(bf16)
            p2_ref[:, lanes] = packed[:, LANES : 2 * LANES]
            p1_ref[:, lanes] = packed[:, 2 * LANES :]


def product_and_states(key_rows, value_rows, rates_t):
    tokens, channels = key_rows.shape
    chunks = 4
    tiles = channels // LANES // chunks
    state_shape = jax.ShapeDtypeStruct((MODES, channels), f32)
    return pl.pallas_call(
        functools.partial(product_kernel, chunks, tiles),
        in_specs=[HBM, HBM, VMEM],
        out_specs=[VMEM] * 6,
        out_shape=[
            jax.ShapeDtypeStruct((CH, channels), bf16),
            state_shape, state_shape, state_shape, jax.ShapeDtypeStruct((MODES, channels), bf16),
            jax.ShapeDtypeStruct((channels // LANES, LANES), f32),
        ],
        scratch_shapes=[
            pltpu.VMEM((tokens, channels), bf16), pltpu.VMEM((tokens, channels), bf16),
            pltpu.SemaphoreType.DMA((2, chunks)),
        ],
        compiler_params=params(56),
        cost_estimate=pl.CostEstimate(
            flops=6 * tokens * channels * CH, bytes_accessed=6 * tokens * channels, transcendentals=channels * CH
        ),
        name="product_states",
    )(key_rows, value_rows, rates_t)


def spread_kernel(rates_ref, out_ref):
    rates = rates_ref[...].T
    high = rates.astype(bf16).astype(f32)
    middle = (rates - high).astype(bf16).astype(f32)
    parts = jnp.concatenate([high, middle, rates - high - middle], axis=1)
    expand = (iota((PER_TILE, LANES), 1) // GW == iota((PER_TILE, LANES), 0)).astype(f32).astype(bf16)
    for t in range(out_ref.shape[1] // LANES):
        wide = tn_dot(parts[t * PER_TILE : (t + 1) * PER_TILE].astype(bf16), expand)
        out_ref[:, t * LANES : (t + 1) * LANES] = wide[:MODES] + wide[MODES : 2 * MODES] + wide[2 * MODES :]


def spread_rates(rates_t):
    return pl.pallas_call(
        spread_kernel,
        out_shape=jax.ShapeDtypeStruct((MODES, rates_t.shape[1] * GW), f32),
        compiler_params=params(),
        name="spread_rates",
    )(rates_t)


FOLD = 4
PARTS = PER_TILE // FOLD


def toeplitz(row):
    return pltpu.roll(jnp.broadcast_to(row, (CH, LANES)), 0, 1, stride=1, stride_axis=0)


def fold_masks():
    group = iota((CH, LANES), 1) // GW
    return [(group % PARTS == a).astype(f32).astype(bf16) for a in range(PARTS)]


def unfold(stacked):
    member = iota((CH, LANES), 1) // GW // PARTS
    out = stacked[:CH]
    for b in range(1, FOLD):
        out = jnp.where(member == b, stacked[b * CH : (b + 1) * CH], out)
    return out


def reversed_lags(taps):
    flip = ((iota((CH, LANES), 0) + iota((CH, LANES), 1)) % CH == 0).astype(f32)
    return jnp.dot(taps, flip, preferred_element_type=f32, precision=highest)


def local_kernel(
    chunks, tiles, k_hbm, v_hbm, taps_ref, rates_ref, coeff_ref, after,
    out_ref, k_ref, v_ref, taps_rev, response, lhs_all, rhs_all, in_sems,
):
    half = PARTS * CH
    width = tiles * LANES
    inputs = [(k_hbm, k_ref, 0, 0), (v_hbm, v_ref, 0, 0)]
    for c in range(chunks):
        for copy in copies(inputs, in_sems, c, width):
            copy.start()
    lag = ((CH - iota((1, LANES), 1)) % CH).astype(f32)
    rates, coeff = rates_ref[...].T, coeff_ref[...].T
    sums = reversed_lags(taps_ref[...])
    taps_rev[...] = sums
    for m in range(MODES):
        sums = sums + coeff[:, m : m + 1] * jnp.exp(-rates[:, m : m + 1] * lag)
    response[...] = sums
    lower = iota((CH, LANES), 1) <= iota((CH, LANES), 0)
    masks = fold_masks()

    @pl.loop(0, chunks)
    def _(c):
        for copy in copies(inputs, in_sems, c, width):
            copy.wait()
        for t in range(tiles):
            lanes = lanes_at(c * tiles + t, LANES)
            lhs_ref, rhs_ref = lhs_all.at[t % 2], rhs_all.at[t % 2]
            x = product_of(k_ref, v_ref, lanes)
            for f in range(PER_TILE):
                a, rows = f % PARTS, slice(f // PARTS * CH, (f // PARTS + 1) * CH)
                row = pl.ds((c * tiles + t) * PER_TILE + f, 1)
                lhs_ref[rows, half + a * CH : half + (a + 1) * CH] = jnp.where(lower, toeplitz(response[row, :]), 0.0).astype(bf16)
                lhs_ref[rows, a * CH : (a + 1) * CH] = jnp.where(lower, 0.0, toeplitz(taps_rev[row, :])).astype(bf16)
            for a in range(PARTS):
                x0, x1, x2 = [x[i * CH : (i + 1) * CH] * masks[a] for i in range(3)]
                rhs_ref[a * CH : (a + 1) * CH, :LANES] = x0
                rhs_ref[a * CH : (a + 1) * CH, LANES:] = x1
                rhs_ref[half + a * CH : half + (a + 1) * CH, :LANES] = x1
                rhs_ref[half + a * CH : half + (a + 1) * CH, LANES:] = x2
            later = jnp.dot(lhs_ref[...], rhs_ref[...], preferred_element_type=f32)
            early = jnp.dot(lhs_ref[:, half:], rhs_ref[:half, :LANES], preferred_element_type=f32)
            out_ref[:CH, lanes] = unfold(early).astype(bf16)
            out_ref[CH : 2 * CH, lanes] = unfold(later[:, :LANES]).astype(bf16)
            out_ref[2 * CH :, lanes] = unfold(later[:, LANES:]).astype(bf16)


def local_part(key_rows, value_rows, taps, rates_t, coeff_t, after):
    tokens, channels = key_rows.shape
    groups = taps.shape[0]
    chunks = 4
    tiles = channels // LANES // chunks
    return pl.pallas_call(
        functools.partial(local_kernel, chunks, tiles),
        in_specs=[HBM, HBM, VMEM, VMEM, VMEM, ANY],
        out_specs=VMEM,
        out_shape=jax.ShapeDtypeStruct((tokens, channels), bf16),
        scratch_shapes=[
            pltpu.VMEM((tokens, channels), bf16), pltpu.VMEM((tokens, channels), bf16),
            pltpu.VMEM((groups, CH), f32), pltpu.VMEM((groups, CH), f32),
            pltpu.VMEM((2, FOLD * CH, 2 * PARTS * CH), bf16), pltpu.VMEM((2, 2 * PARTS * CH, 2 * LANES), bf16),
            pltpu.SemaphoreType.DMA((2, chunks)),
        ],
        compiler_params=params(),
        cost_estimate=pl.CostEstimate(
            flops=groups * CH * 256 * 512 * 2, bytes_accessed=groups * GW * tokens * 4, transcendentals=0
        ),
        name="local_conv",
    )(key_rows, value_rows, taps, rates_t, coeff_t, after)


def cross_of(decays, states):
    mask = same_filter(LANES, len(states) * LANES)
    wide = jnp.concatenate(states, axis=1)
    high = wide.astype(bf16)
    low = wide - high.astype(f32)
    blocks = lambda a: jnp.where(mask, jnp.concatenate([a] * PER_TILE, axis=0), 0.0).astype(bf16)
    stacked = jnp.concatenate([blocks(high.astype(f32)), blocks(low)], axis=0)
    return jnp.dot(jnp.concatenate([decays, decays], axis=1), stacked, preferred_element_type=f32)


def starts_of(lam, weight):
    index = iota((CH, LANES), 0).astype(f32)
    return (weight * jnp.exp(-index * lam)).astype(bf16)


def energy_row(partial):
    return lax.dot_general(
        jnp.ones((8, LANES), f32), partial, (((1,), (1,)), ((), ())), preferred_element_type=f32, precision=highest
    )


def gate_kernel(
    chunks, tiles, local_ref, q_hbm, in_ref, p1_ref, p2_ref, spread_ref, tail_ref, taps_ref, rates_ref, coeff_ref,
    gated_ref, energy_ref, q_ref, weight_ref, taps_rev, lhs_all, total_ref, in_sems,
):
    width = tiles * LANES
    inputs = [(q_hbm, q_ref, 0, 0)]
    for c in range(chunks):
        for copy in copies(inputs, in_sems, c, width):
            copy.start()
    weight_ref[...] = by_tile(coeff_ref[...].T)
    taps_rev[...] = reversed_lags(taps_ref[...])
    total_ref[...] = jnp.zeros_like(total_ref)
    lower = iota((CH, LANES), 1) <= iota((CH, LANES), 0)
    masks = fold_masks()

    @pl.loop(0, chunks)
    def _(c):
        for copy in copies(inputs, in_sems, c, width):
            copy.wait()
        for t in range(tiles):
            lanes = lanes_at(c * tiles + t, LANES)
            lhs_ref = lhs_all.at[t % 2]
            for f in range(PER_TILE):
                a, rows = f % PARTS, slice(f // PARTS * CH, (f // PARTS + 1) * CH)
                at = pl.ds((c * tiles + t) * PER_TILE + f, 1)
                lhs_ref[rows, a * CH : (a + 1) * CH] = jnp.where(lower, 0.0, toeplitz(taps_rev[at, :])).astype(bf16)
            tail = tail_ref[:, lanes]
            masked = jnp.concatenate([tail * mask for mask in masks], axis=0)
            carried = unfold(jnp.dot(lhs_ref[...], masked, preferred_element_type=f32))
            decay = jnp.exp(-float(CH) * spread_ref[:, lanes])
            z0 = in_ref[:, lanes]
            entry = decay * z0
            z1 = entry + p1_ref[:, lanes]
            z2 = decay * entry + p2_ref[:, lanes]
            row = pl.ds(c * tiles + t, 1)
            cross = cross_of(starts_of(rates_ref[row, :], weight_ref[row, :]), [z0, z1, z2])
            for i in range(3):
                rows = slice(i * CH, (i + 1) * CH)
                conv = local_ref[rows, lanes].astype(f32) + cross[:, i * LANES : (i + 1) * LANES]
                if i == 0:
                    conv = conv + carried
                gated = conv * q_ref[rows, lanes].astype(f32)
                gated_ref[rows, lanes] = gated.astype(bf16)
                total_ref[rows] += gated * gated

    energy_ref[...] = energy_row(total_ref[...])


def gate_part(local, query_rows, incoming, p1, p2, rates_spread, tail, taps, rate_rows, coeff_t):
    tokens, channels = local.shape
    chunks = 4
    tiles = channels // LANES // chunks
    return pl.pallas_call(
        functools.partial(gate_kernel, chunks, tiles),
        in_specs=[VMEM, HBM] + [VMEM] * 8,
        out_specs=[VMEM, VMEM],
        out_shape=[jax.ShapeDtypeStruct((tokens, channels), bf16), jax.ShapeDtypeStruct((8, tokens), f32)],
        scratch_shapes=[
            pltpu.VMEM((tokens, channels), bf16), pltpu.VMEM(rate_rows.shape, f32), pltpu.VMEM(taps.shape, f32),
            pltpu.VMEM((2, FOLD * CH, PARTS * CH), bf16), pltpu.VMEM((tokens, LANES), f32),
            pltpu.SemaphoreType.DMA((1, chunks)),
        ],
        compiler_params=params(),
        cost_estimate=pl.CostEstimate(
            flops=channels * CH * 2048, bytes_accessed=channels * tokens * 6, transcendentals=channels * CH
        ),
        name="gate",
    )(local, query_rows, incoming, p1, p2, rates_spread, tail, taps, rate_rows, coeff_t)


def norm_kernel(terms, chunks, tiles, *refs):
    energies, (gated_ref, gain_ref) = refs[:terms], refs[terms : terms + 2]
    out_hbm, out_ref, scale_ref, out_sems = refs[-4:]
    width = tiles * LANES
    rows = gated_ref.shape[0]
    outputs = [(out_ref, out_hbm, 0, 0)]
    energy = sum(ref[...] for ref in energies)
    scale_ref[...] = lax.rsqrt(tn_dot(energy, jnp.full((8, LANES), 0.125, f32), highest) / D + 1e-05)

    @pl.loop(0, chunks)
    def _(c):
        for r in range(0, rows, CH):
            scale = scale_ref[r : r + CH]
            for t in range(tiles):
                lanes = lanes_at(c * tiles + t, LANES)
                value = gated_ref[r : r + CH, lanes].astype(f32) * scale * gain_ref[:, lanes]
                out_ref[r : r + CH, lanes] = value.astype(bf16)
        for copy in copies(outputs, out_sems, c, width):
            copy.start()

    drain(chunks, width, outputs, out_sems)


def norm_part(energies, gated, gain_row):
    rows, channels = gated.shape
    chunks = 4
    tiles = channels // LANES // chunks
    return pl.pallas_call(
        functools.partial(norm_kernel, len(energies), chunks, tiles),
        in_specs=[VMEM] * (len(energies) + 2),
        out_specs=HBM,
        out_shape=jax.ShapeDtypeStruct((rows, channels), bf16),
        scratch_shapes=[
            pltpu.VMEM((rows, channels), bf16), pltpu.VMEM((rows, LANES), f32), pltpu.SemaphoreType.DMA((1, chunks)),
        ],
        compiler_params=params(),
        cost_estimate=pl.CostEstimate(flops=rows * channels * 2, bytes_accessed=rows * channels * 4, transcendentals=0),
        name="norm",
    )(*energies, gated, gain_row)


def regroup(block):
    shape = block.shape
    sub = iota(shape, 1)
    lane = iota(shape, 2) // GW
    for k in (1, 2, 4):
        up = pltpu.roll(pltpu.roll(block, 8 - k, 1), GW * k, 2)
        down = pltpu.roll(pltpu.roll(block, k, 1), LANES - GW * k, 2)
        row_bit, lane_bit = (sub & k) != 0, (lane & k) != 0
        block = jnp.where(row_bit == lane_bit, block, jnp.where(lane_bit, up, down))
    return block


def ranks_of(present):
    count = present.shape[1]
    before = (iota((count, count), 0) < iota((count, count), 1)).astype(bf16)
    return jnp.dot(present.astype(bf16), before, preferred_element_type=f32)


def select_kernel(blocks, slots, inner, outer, me_ref, tail_ref, plan_ref, *refs):
    outs, (items_ref, picks_ref) = refs[:2], refs[2:]
    groups = plan_ref.shape[1]

    @pl.when(me_ref[0] != inner * outer - 1)
    def _():
        for out in outs:
            out[...] = jnp.zeros_like(out)

    @pl.when(me_ref[0] == inner * outer - 1)
    def _():
        for g in range(0, groups // PER_TILE, 2):
            halves = []
            for side in range(2):
                tile = g + side
                rows = tail_ref[:, tile * LANES : (tile + 1) * LANES].astype(f32)
                halves.append(regroup(rows.reshape(2 * blocks, 8, LANES)))
            for b in range(blocks):
                for half in range(2):
                    both = jnp.concatenate([halves[0][2 * b + half], halves[1][2 * b + half]], axis=0)
                    items_ref[
                        b * groups + g * 8 : b * groups + (g + 2) * 8, half * LANES : (half + 1) * LANES
                    ] = both.astype(bf16)
        plan = plan_ref[...]
        readers = iota((inner * outer, 1, 1), 0)
        mine = (plan[None] == readers).astype(f32)
        ranks = ranks_of(jnp.sum(mine, axis=1))
        slot = iota((slots, groups), 0).astype(f32).astype(bf16)
        low = inner // 2
        for o in range(outer):
            for p in range(inner):
                r = o * inner + p
                for b in range(blocks):
                    rank = jnp.where(plan[b : b + 1] == r, ranks[r : r + 1], -1.0)
                    rank = jnp.broadcast_to(rank, (slots, groups)).astype(bf16)
                    picks_ref[p * slots : (p + 1) * slots, b * groups : (b + 1) * groups] = jnp.where(
                        rank == slot, jnp.ones((), bf16), jnp.zeros((), bf16)
                    )
            total = jnp.dot(picks_ref[...], items_ref[...], preferred_element_type=f32)
            total = total.astype(bf16).reshape(2, low, slots, MODES * GW)
            for side in range(2):
                outs[side][o] = total[side]


def select_tails(me, tail, plan_cols, inner, outer, slots):
    rows = tail.shape[0]
    groups = plan_cols.shape[1]
    blocks = rows // MODES
    vmem = pl.BlockSpec(memory_space=pltpu.VMEM)
    return pl.pallas_call(
        functools.partial(select_kernel, blocks, slots, inner, outer),
        in_specs=[pl.BlockSpec(memory_space=pltpu.SMEM), vmem, vmem],
        out_specs=[vmem] * 2,
        out_shape=[jax.ShapeDtypeStruct((outer, inner // 2, slots, MODES * GW), bf16)] * 2,
        scratch_shapes=[
            pltpu.VMEM((blocks * groups, MODES * GW), bf16), pltpu.VMEM((inner * slots, blocks * groups), bf16),
        ],
        compiler_params=params(),
        cost_estimate=pl.CostEstimate(flops=10**9, bytes_accessed=2 * 10**6, transcendentals=0),
        name="select_tails",
    )(me, tail, plan_cols)


def handoff_kernel(me_ref, final_ref, norm_ref, plan_ref, got_ref, out_ref, items_ref):
    groups = plan_ref.shape[1]
    capacity = out_ref.shape[2]
    slots = got_ref.shape[0]
    plan = plan_ref[...]
    mine = plan == me_ref[0]
    present = jnp.sum(mine.astype(f32), axis=0, keepdims=True)
    rank = ranks_of(jnp.broadcast_to(present, (8, groups)))[:1]
    final = final_ref[...] * norm_ref[...]
    stack = [
        final[half * 8 : (half + 1) * 8, g * LANES : (g + 1) * LANES]
        for half in range(2) for g in range(groups // PER_TILE)
    ]
    done = regroup(jnp.stack(stack, axis=0)).reshape(2 * groups, LANES).astype(bf16)
    items_ref[:, :LANES] = done[:groups]
    items_ref[:, LANES:] = done[groups:]
    slot = iota((slots, groups), 0).astype(f32)
    last = plan.shape[0] - 1
    at = (jnp.broadcast_to(rank, (slots, groups)) == slot) & mine[last:]
    pick = jnp.where(at, 1.0, 0.0).astype(bf16)
    rows = jnp.dot(pick, items_ref[...], preferred_element_type=f32)
    rows = (rows + got_ref[...].astype(f32)).T
    out_ref[...] = rows[:, :capacity].reshape(out_ref.shape)


def assemble(me, final, norm_spread, plan_cols, got, capacity):
    groups = plan_cols.shape[1]
    vmem = pl.BlockSpec(memory_space=pltpu.VMEM)
    out = pl.pallas_call(
        handoff_kernel,
        in_specs=[pl.BlockSpec(memory_space=pltpu.SMEM), vmem, vmem, vmem, vmem],
        out_specs=vmem,
        out_shape=jax.ShapeDtypeStruct((MODES, GW, capacity), f32),
        scratch_shapes=[pltpu.VMEM((groups, MODES * GW), bf16)],
        compiler_params=params(),
        cost_estimate=pl.CostEstimate(flops=10**9, bytes_accessed=10**6, transcendentals=0),
        name="handoff",
    )(me, final, norm_spread, plan_cols, got)
    return out.transpose(2, 0, 1)


def hold_kernel(*refs):
    pass


def hold(array, after):
    anywhere = pl.BlockSpec(memory_space=pl.ANY)
    return pl.pallas_call(
        hold_kernel,
        in_specs=[anywhere, anywhere],
        out_specs=anywhere,
        out_shape=jax.ShapeDtypeStruct(array.shape, array.dtype),
        input_output_aliases={0: 0},
        name="hold",
    )(array, after)


def scatter_tails(selected, inner, outer):
    count = inner * outer
    me = lax.axis_index("seq")
    half = inner // 2
    low, high = selected
    sent = lax.ppermute(low, "seq", [(count - 1, count - 1 - half)])
    block = jnp.where((me & half) != 0, high, sent)
    heads = [half - 1, inner - 1]
    own = block[outer - 1]
    for o in range(outer - 1):
        pairs = [(count - inner + h, o * inner + h) for h in heads]
        sent = lax.ppermute(block[o], "seq", pairs)
        own = jnp.where(me // inner == o, sent, own)
    half //= 2
    while half:
        pairs = [(i, i - half) for i in range(count) if (i + 1) % (2 * half) == 0]
        sent = lax.ppermute(own[:half], "seq", pairs)
        own = jnp.where((me & half) != 0, own[half:], sent)
        half //= 2
    return own[0]


def scan_states(own, sent, rates_spread, tokens):
    count = lax.axis_size("seq")
    me = lax.axis_index("seq")
    total, incoming = own, jnp.zeros_like(own)
    stages = []
    step = 1
    while step < count:
        pairs = [(i, i ^ step) for i in range(count)]
        other = lax.ppermute(sent, "seq", pairs).astype(f32)
        right = (me & step) != 0
        offset = ((me & (step - 1)) * tokens).astype(f32)
        incoming = jnp.where(right, incoming + jnp.exp(-rates_spread * offset) * other, incoming)
        decay = jnp.exp(-rates_spread * float(step * tokens))
        total = jnp.where(right, decay * other + total, decay * total + other)
        sent = total.astype(bf16)
        stages.append(sent)
        step *= 2
    return total, incoming, stages


def sum_over_chan(energy):
    if lax.axis_size("chan") == 2:
        return [energy, lax.ppermute(energy, "chan", [(0, 1), (1, 0)])]
    return [lax.psum(energy, "chan")]


def per_device(
    query_rows, key_rows, value_rows, residues, decay_rates, medium_taps, out_gain, reader_plan
):
    tokens, channels = query_rows.shape
    groups, mode_count = residues.shape
    blocks = medium_taps.shape[1] // mode_count
    seq_count = lax.axis_size("seq")
    me = lax.axis_index("seq")

    rates_t = decay_rates.T
    own_tail, p1, p2, own, sent, rate_rows = product_and_states(key_rows, value_rows, rates_t)
    rates_spread = spread_rates(rates_t)
    total, incoming, stages = scan_states(own, sent, rates_spread, tokens)
    onward = [(i, i + 1) for i in range(seq_count - 1)]
    tail_prev = lax.ppermute(hold(own_tail, stages[0]), "seq", onward)

    coeff_t = residues.T * jnp.sqrt(-jnp.expm1(-2.0 * rates_t))
    norm_spread = jnp.sqrt(-jnp.expm1(-2.0 * rates_spread))
    plan_cols = reader_plan.T

    inner = 1 << (int(math.log2(seq_count)) // 2)
    outer = seq_count // inner
    capacity = (groups * (blocks + 1) + seq_count - 1) // seq_count + 1
    slots = -(-capacity // 16) * 16
    selected = select_tails(me.reshape(1), own_tail, plan_cols, inner, outer, slots)
    got = scatter_tails(selected, inner, outer)

    local = local_part(key_rows, value_rows, medium_taps, rates_t, coeff_t, stages[0])
    gated, energy = gate_part(
        local, query_rows, incoming, p1, p2, rates_spread, tail_prev, medium_taps, rate_rows, coeff_t
    )
    mixed = norm_part(sum_over_chan(energy), gated, out_gain[None, :])
    handoff = assemble(me.reshape(1), total, norm_spread, plan_cols, got, capacity)
    return mixed, handoff


def solution(mesh):
    placed = (
        P("seq", "chan"),
        P("seq", "chan"),
        P("seq", "chan"),
        P("chan", None),
        P("chan", None),
        P("chan", None),
        P("chan"),
        P("chan", None),
    )
    return jax.shard_map(
        per_device,
        mesh=mesh,
        in_specs=placed,
        out_specs=(P("seq", "chan"), P("seq", None, "chan")),
        check_vma=False,
    )
```

```python
import functools
import math

import jax
import jax.numpy as jnp
from jax import lax
from jax.experimental import pallas as pl
from jax.experimental.pallas import tpu as pltpu
from jax.sharding import PartitionSpec as P

D = 8192
GW = 16
MODES = 16
CH = 128
LANES = 128
PER_TILE = LANES // GW
f32 = jnp.float32
bf16 = jnp.bfloat16
highest = lax.Precision.HIGHEST


def params(mib=20):
    return pltpu.CompilerParams(vmem_limit_bytes=mib * 1024 * 1024)


def iota(shape, axis):
    return lax.broadcasted_iota(jnp.int32, shape, axis)


def same_filter(rows, lanes):
    return (iota((rows, lanes), 0) // MODES) == ((iota((rows, lanes), 1) % LANES) // GW)


def tn_dot(a, b, precision=None):
    return lax.dot_general(
        a, b, (((0,), (0,)), ((), ())), preferred_element_type=f32, precision=precision
    )


def by_tile(values):
    groups = values.shape[0]
    copies = (iota((MODES, LANES), 1) % MODES == iota((MODES, LANES), 0)).astype(f32)
    wide = jnp.dot(values, copies, preferred_element_type=f32, precision=highest)
    mine = (iota((groups, LANES), 1) // MODES) == (iota((groups, LANES), 0) % PER_TILE)
    return jnp.where(mine, wide, 0.0).reshape(groups // PER_TILE, PER_TILE, LANES).sum(axis=1)


ANY = pl.BlockSpec(memory_space=pl.ANY)
VMEM = pl.BlockSpec(memory_space=pltpu.VMEM)
HBM = pl.BlockSpec(memory_space=pltpu.HBM)
SMEM = pl.BlockSpec(memory_space=pltpu.SMEM)
TOKEN = jax.ShapeDtypeStruct((8, 128), jnp.float32)


def lanes_at(index, width):
    return pl.ds(pl.multiple_of(index * width, width), width)


def copies(pairs, sems, chunk, width):
    out = []
    for i, (source, target, from_lane, to_lane) in enumerate(pairs):
        out.append(
            pltpu.make_async_copy(
                source.at[:, pl.ds(pl.multiple_of(from_lane + chunk * width, LANES), width)],
                target.at[:, pl.ds(pl.multiple_of(to_lane + chunk * width, LANES), width)],
                sems.at[i, chunk],
            )
        )
    return out


def drain(chunks, width, outputs, out_sems):
    for c in range(chunks):
        for copy in copies(outputs, out_sems, c, width):
            copy.wait()


def product_of(k_ref, v_ref, lanes):
    return (k_ref[:, lanes].astype(f32) * v_ref[:, lanes].astype(f32)).astype(bf16)


def product_kernel(
    chunks, tiles, k_hbm, v_hbm, rates_ref, tail_hbm, p1_hbm, p2_hbm, own_hbm, sent_hbm, rows_ref,
    k_ref, v_ref, tail_ref, p1_ref, p2_ref, own_ref, sent_ref, in_sems, out_sems,
):
    width = tiles * LANES
    inputs = [(k_hbm, k_ref, 0, 0), (v_hbm, v_ref, 0, 0)]
    outputs = [
        (sent_ref, sent_hbm, 0, 0), (own_ref, own_hbm, 0, 0), (tail_ref, tail_hbm, 0, 0),
        (p1_ref, p1_hbm, 0, 0), (p2_ref, p2_hbm, 0, 0),
    ]
    for c in range(chunks):
        for copy in copies(inputs, in_sems, c, width):
            copy.start()
    rows_ref[...] = by_tile(rates_ref[...].T)
    to_end = (CH - iota((CH, LANES), 0)).astype(f32)
    mask = same_filter(LANES, 3 * LANES)
    none = jnp.zeros((CH, LANES), bf16)

    @pl.loop(0, chunks)
    def _(c):
        for copy in copies(inputs, in_sems, c, width):
            copy.wait()
        for t in range(tiles):
            lanes = lanes_at(c * tiles + t, LANES)
            x = product_of(k_ref, v_ref, lanes)
            tail_ref[:, lanes] = x[2 * CH :]
            lam = rows_ref[pl.ds(c * tiles + t, 1), :]
            near = jnp.exp(-to_end * lam)
            decay = jnp.exp(-float(CH) * lam)
            middle = near * decay
            ends = jnp.concatenate([(middle * decay).astype(bf16), middle.astype(bf16), near.astype(bf16)], axis=0)
            x0, x1 = x[:CH], x[CH : 2 * CH]
            wide = jnp.concatenate(
                [x, jnp.concatenate([none, x0, x1], axis=0), jnp.concatenate([none, none, x0], axis=0)], axis=1
            )
            full = tn_dot(ends, wide)
            packed = jnp.where(mask, full, 0.0).reshape(PER_TILE, MODES, 3 * LANES).sum(axis=0)
            own_ref[:, lanes] = packed[:, :LANES]
            sent_ref[:, lanes] = packed[:, :LANES].astype(bf16)
            p2_ref[:, lanes] = packed[:, LANES : 2 * LANES]
            p1_ref[:, lanes] = packed[:, 2 * LANES :]
        for copy in copies(outputs, out_sems, c, width):
            copy.start()

    drain(chunks, width, outputs, out_sems)


def product_and_states(key_rows, value_rows, rates_t):
    tokens, channels = key_rows.shape
    chunks = min(8, channels // LANES // 2)
    tiles = channels // LANES // chunks
    state_shape = jax.ShapeDtypeStruct((MODES, channels), f32)
    return pl.pallas_call(
        functools.partial(product_kernel, chunks, tiles),
        in_specs=[HBM, HBM, VMEM],
        out_specs=[ANY] * 5 + [VMEM],
        out_shape=[
            jax.ShapeDtypeStruct((CH, channels), bf16),
            state_shape, state_shape, state_shape, jax.ShapeDtypeStruct((MODES, channels), bf16),
            jax.ShapeDtypeStruct((channels // LANES, LANES), f32),
        ],
        scratch_shapes=[
            pltpu.VMEM((tokens, channels), bf16), pltpu.VMEM((tokens, channels), bf16), pltpu.VMEM((CH, channels), bf16),
            pltpu.VMEM((MODES, channels), f32), pltpu.VMEM((MODES, channels), f32), pltpu.VMEM((MODES, channels), f32),
            pltpu.VMEM((MODES, channels), bf16),
            pltpu.SemaphoreType.DMA((2, chunks)), pltpu.SemaphoreType.DMA((5, chunks)),
        ],
        compiler_params=params(56),
        cost_estimate=pl.CostEstimate(
            flops=6 * tokens * channels * CH, bytes_accessed=6 * tokens * channels, transcendentals=channels * CH
        ),
        name="product_states",
    )(key_rows, value_rows, rates_t)


FOLD = 4
PARTS = PER_TILE // FOLD


def toeplitz(row):
    return pltpu.roll(jnp.broadcast_to(row, (CH, LANES)), 0, 1, stride=1, stride_axis=0)


def fold_masks():
    group = iota((CH, LANES), 1) // GW
    return [(group % PARTS == a).astype(f32).astype(bf16) for a in range(PARTS)]


def unfold(stacked):
    member = iota((CH, LANES), 1) // GW // PARTS
    out = stacked[:CH]
    for b in range(1, FOLD):
        out = jnp.where(member == b, stacked[b * CH : (b + 1) * CH], out)
    return out


def reversed_lags(taps):
    flip = ((iota((CH, LANES), 0) + iota((CH, LANES), 1)) % CH == 0).astype(f32)
    return jnp.dot(taps, flip, preferred_element_type=f32, precision=highest)


def local_kernel(
    chunks, tiles, k_hbm, v_hbm, taps_rev, response, after,
    out_ref, token_ref, k_ref, v_ref, lhs_all, rhs_all, in_sems,
):
    token_ref[...] = jnp.zeros_like(token_ref)
    half = PARTS * CH
    width = tiles * LANES
    inputs = [(k_hbm, k_ref, 0, 0), (v_hbm, v_ref, 0, 0)]
    for c in range(chunks):
        for copy in copies(inputs, in_sems, c, width):
            copy.start()
    lower = iota((CH, LANES), 1) <= iota((CH, LANES), 0)
    masks = fold_masks()

    @pl.loop(0, chunks)
    def _(c):
        for copy in copies(inputs, in_sems, c, width):
            copy.wait()
        for t in range(tiles):
            lanes = lanes_at(c * tiles + t, LANES)
            lhs_ref, rhs_ref = lhs_all.at[t % 2], rhs_all.at[t % 2]
            x = product_of(k_ref, v_ref, lanes)
            for f in range(PER_TILE):
                a, rows = f % PARTS, slice(f // PARTS * CH, (f // PARTS + 1) * CH)
                row = pl.ds((c * tiles + t) * PER_TILE + f, 1)
                lhs_ref[rows, half + a * CH : half + (a + 1) * CH] = jnp.where(lower, toeplitz(response[row, :]), 0.0).astype(bf16)
                lhs_ref[rows, a * CH : (a + 1) * CH] = jnp.where(lower, 0.0, toeplitz(taps_rev[row, :])).astype(bf16)
            for a in range(PARTS):
                x0, x1, x2 = [x[i * CH : (i + 1) * CH] * masks[a] for i in range(3)]
                rhs_ref[a * CH : (a + 1) * CH, :LANES] = x0
                rhs_ref[a * CH : (a + 1) * CH, LANES:] = x1
                rhs_ref[half + a * CH : half + (a + 1) * CH, :LANES] = x1
                rhs_ref[half + a * CH : half + (a + 1) * CH, LANES:] = x2
            later = jnp.dot(lhs_ref[...], rhs_ref[...], preferred_element_type=f32)
            early = jnp.dot(lhs_ref[:, half:], rhs_ref[:half, :LANES], preferred_element_type=f32)
            out_ref[:CH, lanes] = unfold(early).astype(bf16)
            out_ref[CH : 2 * CH, lanes] = unfold(later[:, :LANES]).astype(bf16)
            out_ref[2 * CH :, lanes] = unfold(later[:, LANES:]).astype(bf16)


def local_part(key_rows, value_rows, taps_rev, response, after):
    tokens, channels = key_rows.shape
    groups = taps_rev.shape[0]
    chunks = 4
    tiles = channels // LANES // chunks
    return pl.pallas_call(
        functools.partial(local_kernel, chunks, tiles),
        in_specs=[ANY, ANY, VMEM, VMEM, ANY],
        out_specs=[VMEM, VMEM],
        out_shape=[jax.ShapeDtypeStruct((tokens, channels), bf16), TOKEN],
        scratch_shapes=[pltpu.VMEM((tokens, channels), bf16)] * 2 + [
            pltpu.VMEM((2, FOLD * CH, 2 * PARTS * CH), bf16), pltpu.VMEM((2, 2 * PARTS * CH, 2 * LANES), bf16),
            pltpu.SemaphoreType.DMA((2, chunks)),
        ],
        compiler_params=params(),
        cost_estimate=pl.CostEstimate(
            flops=groups * CH * 256 * 512 * 2, bytes_accessed=groups * GW * tokens * 4, transcendentals=0
        ),
        name="local_conv",
    )(key_rows, value_rows, taps_rev, response, after)


def carry_kernel(
    chunks, tiles, local_ref, tail_ref, taps_rev, q_hbm, p1_hbm, p2_hbm, weight_hbm, after,
    out_ref, token_ref, q_ref, p1_ref, p2_ref, weight_ref, lhs_all, sems,
):
    bring = [
        pltpu.make_async_copy(source, target, sems.at[i])
        for i, (source, target) in enumerate(
            [(q_hbm, q_ref), (p1_hbm, p1_ref), (p2_hbm, p2_ref), (weight_hbm, weight_ref)]
        )
    ]
    for copy in bring:
        copy.start()
    token_ref[...] = jnp.zeros_like(token_ref)
    lower = iota((CH, LANES), 1) <= iota((CH, LANES), 0)
    masks = fold_masks()

    @pl.loop(0, chunks)
    def _(c):
        for t in range(tiles):
            lanes = lanes_at(c * tiles + t, LANES)
            lhs_ref = lhs_all.at[t % 2]
            for f in range(PER_TILE):
                a, rows = f % PARTS, slice(f // PARTS * CH, (f // PARTS + 1) * CH)
                at = pl.ds((c * tiles + t) * PER_TILE + f, 1)
                lhs_ref[rows, a * CH : (a + 1) * CH] = jnp.where(lower, 0.0, toeplitz(taps_rev[at, :])).astype(bf16)
            tail = tail_ref[:, lanes]
            masked = jnp.concatenate([tail * mask for mask in masks], axis=0)
            carried = unfold(jnp.dot(lhs_ref[...], masked, preferred_element_type=f32))
            out_ref[:, lanes] = (local_ref[:CH, lanes].astype(f32) + carried).astype(bf16)

    for copy in bring:
        copy.wait()


def carry_part(local, tail, taps_rev, query_rows, p1, p2, weight_rows, after):
    tokens, channels = local.shape
    chunks = 4
    tiles = channels // LANES // chunks
    return pl.pallas_call(
        functools.partial(carry_kernel, chunks, tiles),
        in_specs=[VMEM, VMEM, VMEM] + [ANY] * 5,
        out_specs=[VMEM] * 6,
        out_shape=[jax.ShapeDtypeStruct((CH, channels), bf16), TOKEN]
        + [jax.ShapeDtypeStruct(a.shape, a.dtype) for a in (query_rows, p1, p2, weight_rows)],
        scratch_shapes=[pltpu.VMEM((2, FOLD * CH, PARTS * CH), bf16), pltpu.SemaphoreType.DMA((4,))],
        compiler_params=params(),
        cost_estimate=pl.CostEstimate(flops=channels * CH * 1024, bytes_accessed=channels * CH * 6, transcendentals=0),
        name="carry",
    )(local, tail, taps_rev, query_rows, p1, p2, weight_rows, after)


def exact_parts(values):
    high = values.astype(bf16).astype(f32)
    middle = (values - high).astype(bf16).astype(f32)
    return jnp.concatenate([high, middle, values - high - middle], axis=1)


def prepare_kernel(
    rates_ref, factor_ref, residues_ref, taps_ref, spread_ref, norm_ref, taps_rev_ref, response_ref, weight_ref
):
    rates, factor = rates_ref[...].T, factor_ref[...].T
    coeff = residues_ref[...].T * factor
    expand = (iota((PER_TILE, LANES), 1) // GW == iota((PER_TILE, LANES), 0)).astype(f32).astype(bf16)
    for source, target in ((exact_parts(rates), spread_ref), (exact_parts(factor), norm_ref)):
        for t in range(target.shape[1] // LANES):
            wide = tn_dot(source[t * PER_TILE : (t + 1) * PER_TILE].astype(bf16), expand)
            target[:, t * LANES : (t + 1) * LANES] = wide[:MODES] + wide[MODES : 2 * MODES] + wide[2 * MODES :]
    weight_ref[...] = by_tile(coeff)
    lag = ((CH - iota((1, LANES), 1)) % CH).astype(f32)
    sums = reversed_lags(taps_ref[...])
    taps_rev_ref[...] = sums
    for m in range(MODES):
        sums = sums + coeff[:, m : m + 1] * jnp.exp(-rates[:, m : m + 1] * lag)
    response_ref[...] = sums


def prepare(rates_t, factor_t, residues_t, taps):
    groups = taps.shape[0]
    shapes = [(MODES, groups * GW), (MODES, groups * GW), taps.shape, taps.shape, (groups // PER_TILE, LANES)]
    return pl.pallas_call(
        prepare_kernel,
        in_specs=[VMEM] * 4,
        out_specs=[VMEM] * 5,
        out_shape=[jax.ShapeDtypeStruct(shape, f32) for shape in shapes],
        compiler_params=params(),
        name="prepare",
    )(rates_t, factor_t, residues_t, taps)


def cross_of(decays, states):
    mask = same_filter(LANES, len(states) * LANES)
    wide = jnp.concatenate(states, axis=1)
    high = wide.astype(bf16)
    low = wide - high.astype(f32)
    blocks = lambda a: jnp.where(mask, jnp.concatenate([a] * PER_TILE, axis=0), 0.0).astype(bf16)
    stacked = jnp.concatenate([blocks(high.astype(f32)), blocks(low)], axis=0)
    return jnp.dot(jnp.concatenate([decays, decays], axis=1), stacked, preferred_element_type=f32)


def starts_of(lam, weight):
    index = iota((CH, LANES), 0).astype(f32)
    return (weight * jnp.exp(-index * lam)).astype(bf16)


def energy_row(partial):
    return lax.dot_general(
        jnp.ones((8, LANES), f32), partial, (((1,), (1,)), ((), ())), preferred_element_type=f32, precision=highest
    )


def gate_kernel(
    chunks, tiles, step, me_ref, first_ref, local_ref, q_ref, in_ref, other_ref, p1_ref, p2_ref, spread_ref, rates_ref, weight_ref,
    gated_ref, energy_ref, total_ref,
):
    me = me_ref[0]
    offset = ((me & (step - 1)) * gated_ref.shape[0]).astype(f32)
    right = jnp.where((me & step) != 0, 1.0, 0.0)
    total_ref[...] = jnp.zeros_like(total_ref)

    @pl.loop(0, chunks)
    def _(c):
        for t in range(tiles):
            lanes = lanes_at(c * tiles + t, LANES)
            spread = spread_ref[:, lanes]
            decay = jnp.exp(-float(CH) * spread)
            z0 = in_ref[:, lanes] + right * (jnp.exp(-spread * offset) * other_ref[:, lanes].astype(f32))
            entry = decay * z0
            z1 = entry + p1_ref[:, lanes]
            z2 = decay * entry + p2_ref[:, lanes]
            row = pl.ds(c * tiles + t, 1)
            cross = cross_of(starts_of(rates_ref[row, :], weight_ref[row, :]), [z0, z1, z2])
            for i in range(3):
                rows = slice(i * CH, (i + 1) * CH)
                own = first_ref[:, lanes] if i == 0 else local_ref[rows, lanes]
                gated = (own.astype(f32) + cross[:, i * LANES : (i + 1) * LANES]) * q_ref[rows, lanes].astype(f32)
                gated_ref[rows, lanes] = gated.astype(bf16)
                total_ref[rows] += gated * gated

    energy_ref[...] = energy_row(total_ref[...])


def gate_part(me, step, first, local, query_rows, incoming, other, p1, p2, rates_spread, rate_rows, weight_rows):
    tokens, channels = query_rows.shape
    chunks = 4
    tiles = channels // LANES // chunks
    return pl.pallas_call(
        functools.partial(gate_kernel, chunks, tiles, step),
        in_specs=[SMEM] + [VMEM] * 10,
        out_specs=[VMEM, VMEM],
        out_shape=[
            jax.ShapeDtypeStruct((tokens, channels), bf16), jax.ShapeDtypeStruct((8, tokens), f32),
        ],
        scratch_shapes=[pltpu.VMEM((tokens, LANES), f32)],
        compiler_params=params(),
        cost_estimate=pl.CostEstimate(
            flops=channels * CH * 2048, bytes_accessed=channels * tokens * 6, transcendentals=channels * CH
        ),
        name="gate",
    )(me, first, local, query_rows, incoming, other, p1, p2, rates_spread, rate_rows, weight_rows)


def norm_kernel(terms, chunks, tiles, *refs):
    energies, (gated_ref, gain_ref) = refs[:terms], refs[terms : terms + 2]
    out_hbm, token_ref, out_ref, scale_ref, out_sems = refs[-5:]
    token_ref[...] = jnp.zeros_like(token_ref)
    width = tiles * LANES
    rows = gated_ref.shape[0]
    outputs = [(out_ref, out_hbm, 0, 0)]
    energy = sum(ref[...] for ref in energies)
    scale_ref[...] = lax.rsqrt(tn_dot(energy, jnp.full((8, LANES), 0.125, f32), highest) / D + 1e-05)

    @pl.loop(0, chunks)
    def _(c):
        for r in range(0, rows, CH):
            scale = scale_ref[r : r + CH]
            for t in range(tiles):
                lanes = lanes_at(c * tiles + t, LANES)
                value = gated_ref[r : r + CH, lanes].astype(f32) * scale * gain_ref[:, lanes]
                out_ref[r : r + CH, lanes] = value.astype(bf16)
        for copy in copies(outputs, out_sems, c, width):
            copy.start()

    drain(chunks, width, outputs, out_sems)


def norm_part(energies, gated, gain_row):
    rows, channels = gated.shape
    chunks = 4
    tiles = channels // LANES // chunks
    return pl.pallas_call(
        functools.partial(norm_kernel, len(energies), chunks, tiles),
        in_specs=[VMEM] * (len(energies) + 2),
        out_specs=[HBM, VMEM],
        out_shape=[jax.ShapeDtypeStruct((rows, channels), bf16), TOKEN],
        scratch_shapes=[
            pltpu.VMEM((rows, channels), bf16), pltpu.VMEM((rows, LANES), f32), pltpu.SemaphoreType.DMA((1, chunks)),
        ],
        compiler_params=params(),
        cost_estimate=pl.CostEstimate(flops=rows * channels * 2, bytes_accessed=rows * channels * 4, transcendentals=0),
        name="norm",
    )(*energies, gated, gain_row)


def regroup(block):
    shape = block.shape
    sub = iota(shape, 1)
    lane = iota(shape, 2) // GW
    for k in (1, 2, 4):
        up = pltpu.roll(pltpu.roll(block, 8 - k, 1), GW * k, 2)
        down = pltpu.roll(pltpu.roll(block, k, 1), LANES - GW * k, 2)
        row_bit, lane_bit = (sub & k) != 0, (lane & k) != 0
        block = jnp.where(row_bit == lane_bit, block, jnp.where(lane_bit, up, down))
    return block


def ranks_of(present):
    count = present.shape[1]
    before = (iota((count, count), 0) < iota((count, count), 1)).astype(bf16)
    return jnp.dot(present.astype(bf16), before, preferred_element_type=f32)


def select_kernel(blocks, slots, inner, outer, me_ref, tail_hbm, plan_ref, *refs):
    outs, (items_ref, picks_ref, tail_ref, sem) = refs[:2], refs[2:]
    groups = plan_ref.shape[1]

    @pl.when(me_ref[0] != inner * outer - 1)
    def _():
        for out in outs:
            out[...] = jnp.zeros_like(out)

    @pl.when(me_ref[0] == inner * outer - 1)
    def _():
        copy = pltpu.make_async_copy(tail_hbm, tail_ref, sem)
        copy.start()
        copy.wait()
        for g in range(0, groups // PER_TILE, 2):
            halves = []
            for side in range(2):
                tile = g + side
                rows = tail_ref[:, tile * LANES : (tile + 1) * LANES].astype(f32)
                halves.append(regroup(rows.reshape(2 * blocks, 8, LANES)))
            for b in range(blocks):
                for half in range(2):
                    both = jnp.concatenate([halves[0][2 * b + half], halves[1][2 * b + half]], axis=0)
                    items_ref[
                        b * groups + g * 8 : b * groups + (g + 2) * 8, half * LANES : (half + 1) * LANES
                    ] = both.astype(bf16)
        plan = plan_ref[...]
        readers = iota((inner * outer, 1, 1), 0)
        mine = (plan[None] == readers).astype(f32)
        ranks = ranks_of(jnp.sum(mine, axis=1))
        slot = iota((slots, groups), 0).astype(f32).astype(bf16)
        low = inner // 2
        for o in range(outer):
            for p in range(inner):
                r = o * inner + p
                for b in range(blocks):
                    rank = jnp.where(plan[b : b + 1] == r, ranks[r : r + 1], -1.0)
                    rank = jnp.broadcast_to(rank, (slots, groups)).astype(bf16)
                    picks_ref[p * slots : (p + 1) * slots, b * groups : (b + 1) * groups] = jnp.where(
                        rank == slot, jnp.ones((), bf16), jnp.zeros((), bf16)
                    )
            total = jnp.dot(picks_ref[...], items_ref[...], preferred_element_type=f32)
            total = total.astype(bf16).reshape(2, low, slots, MODES * GW)
            for side in range(2):
                outs[side][o] = total[side]


def select_tails(me, tail, plan_cols, inner, outer, slots):
    rows = tail.shape[0]
    groups = plan_cols.shape[1]
    blocks = rows // MODES
    vmem = pl.BlockSpec(memory_space=pltpu.VMEM)
    return pl.pallas_call(
        functools.partial(select_kernel, blocks, slots, inner, outer),
        in_specs=[SMEM, ANY, vmem],
        out_specs=[vmem, vmem],
        out_shape=[jax.ShapeDtypeStruct((outer, inner // 2, slots, MODES * GW), bf16)] * 2,
        scratch_shapes=[
            pltpu.VMEM((blocks * groups, MODES * GW), bf16), pltpu.VMEM((inner * slots, blocks * groups), bf16),
            pltpu.VMEM(tail.shape, bf16), pltpu.SemaphoreType.DMA,
        ],
        compiler_params=params(56),
        cost_estimate=pl.CostEstimate(flops=10**9, bytes_accessed=2 * 10**6, transcendentals=0),
        name="select_tails",
    )(me, tail, plan_cols)


def handoff_kernel(step, tokens, me_ref, total_ref, other_ref, spread_ref, norm_ref, plan_ref, kept_ref, sent_ref, after, out_ref, items_ref):
    groups = plan_ref.shape[1]
    capacity = out_ref.shape[2]
    slots = sent_ref.shape[0]
    kept = me_ref[0] % 2 == 1
    plan = plan_ref[...]
    mine = plan == me_ref[0]
    present = jnp.sum(mine.astype(f32), axis=0, keepdims=True)
    rank = ranks_of(jnp.broadcast_to(present, (8, groups)))[:1]
    total, other = total_ref[...], other_ref[...].astype(f32)
    right = (me_ref[0] & step) != 0
    earlier, later = jnp.where(right, other, total), jnp.where(right, total, other)
    final = (jnp.exp(-spread_ref[...] * float(step * tokens)) * earlier + later) * norm_ref[...]
    stack = [
        final[half * 8 : (half + 1) * 8, g * LANES : (g + 1) * LANES]
        for half in range(2) for g in range(groups // PER_TILE)
    ]
    done = regroup(jnp.stack(stack, axis=0)).reshape(2 * groups, LANES).astype(bf16)
    items_ref[:, :LANES] = done[:groups]
    items_ref[:, LANES:] = done[groups:]
    slot = iota((slots, groups), 0).astype(f32)
    last = plan.shape[0] - 1
    at = (jnp.broadcast_to(rank, (slots, groups)) == slot) & mine[last:]
    pick = jnp.where(at, 1.0, 0.0).astype(bf16)
    rows = jnp.dot(pick, items_ref[...], preferred_element_type=f32)
    rows = (rows + jnp.where(kept, kept_ref[...].astype(f32), sent_ref[...].astype(f32))).T
    out_ref[...] = rows[:, :capacity].reshape(out_ref.shape)


def assemble(me, step, tokens, total, other, rates_spread, norm_spread, plan_cols, kept, sent, capacity, after):
    groups = plan_cols.shape[1]
    vmem = pl.BlockSpec(memory_space=pltpu.VMEM)
    out = pl.pallas_call(
        functools.partial(handoff_kernel, step, tokens),
        in_specs=[SMEM] + [vmem] * 7 + [ANY],
        out_specs=vmem,
        out_shape=jax.ShapeDtypeStruct((MODES, GW, capacity), f32),
        scratch_shapes=[pltpu.VMEM((groups, MODES * GW), bf16)],
        compiler_params=params(),
        cost_estimate=pl.CostEstimate(flops=10**9, bytes_accessed=10**6, transcendentals=0),
        name="handoff",
    )(me, total, other, rates_spread, norm_spread, plan_cols, kept, sent, after)
    return out.transpose(2, 0, 1)


def hold_kernel(*refs):
    pass


def hold(array, *after):
    return pl.pallas_call(
        hold_kernel,
        in_specs=[ANY] * (1 + len(after)),
        out_specs=ANY,
        out_shape=jax.ShapeDtypeStruct(array.shape, array.dtype),
        input_output_aliases={0: 0},
        name="hold",
    )(array, *after)


def scatter_high(low, high, inner, outer, token):
    count = inner * outer
    sent = lax.ppermute(low, "seq", [(count - 1, count - 1 - inner // 2)])
    return jnp.where((lax.axis_index("seq") & (inner // 2)) != 0, high, sent + token[0, 0].astype(bf16))


def scatter_outer(block, inner, outer):
    base = inner * (outer - 1)
    heads = (inner // 2 - 1, inner - 1)
    return [
        lax.ppermute(block[o], "seq", [(base + h, o * inner + h) for h in heads]) for o in range(outer - 1)
    ]


def scatter_low(own, inner, outer):
    half = inner // 4
    while True:
        pairs = [(i, i - half) for i in range(inner * outer) if (i + 1) % (2 * half) == 0]
        sent = lax.ppermute(own[:half], "seq", pairs)
        if half == 1:
            return own[1], sent[0]
        own = jnp.where((lax.axis_index("seq") & half) != 0, own[half:], sent)
        half //= 2


def exchange(sent, count, inner, step):
    pairs = [(i, i ^ step) for i in range(count)]
    if step != inner:
        return [lax.ppermute(sent, "seq", pairs)]
    last = lambda i: i % inner == inner - 1
    main = [(i, j) for i, j in pairs if not (last(i) and j > i)]
    extra = [(i - inner // 2, j) for i, j in pairs if last(i) and j > i]
    return [lax.ppermute(sent, "seq", main), lax.ppermute(sent, "seq", extra)]


def scan_states(own, sent, rates_spread, tokens, inner, beside):
    count = lax.axis_size("seq")
    me = lax.axis_index("seq")
    total, incoming = own, jnp.zeros_like(own)
    step = 1
    while True:
        got = exchange(sent, count, inner, step)
        if beside:
            beside.pop(0)(sent)
        if 2 * step >= count:
            return total, incoming, functools.reduce(jnp.add, got), step
        other = sum(part.astype(f32) for part in got)
        right = (me & step) != 0
        offset = ((me & (step - 1)) * tokens).astype(f32)
        decay = jnp.exp(-rates_spread * float(step * tokens))
        total = jnp.where(right, decay * other + total, decay * total + other)
        incoming = jnp.where(right, incoming + jnp.exp(-rates_spread * offset) * other, incoming)
        sent = total.astype(bf16)
        step *= 2


def sum_over_chan(energy):
    if lax.axis_size("chan") == 2:
        return [energy, lax.ppermute(energy, "chan", [(0, 1), (1, 0)])]
    return [lax.psum(energy, "chan")]


def per_device(
    query_rows, key_rows, value_rows, residues, decay_rates, medium_taps, out_gain, reader_plan
):
    tokens, channels = query_rows.shape
    groups, mode_count = residues.shape
    blocks = medium_taps.shape[1] // mode_count
    seq_count = lax.axis_size("seq")
    me = lax.axis_index("seq")

    rates_t = decay_rates.T
    factor_t = jnp.sqrt(-jnp.expm1(-2.0 * rates_t))
    own_tail, p1, p2, own, sent, rate_rows = product_and_states(key_rows, value_rows, rates_t)
    rates_spread, norm_spread, taps_rev, response, weight_rows = prepare(rates_t, factor_t, residues.T, medium_taps)
    inner = 1 << (int(math.log2(seq_count)) // 2)
    outer = seq_count // inner

    plan_cols = reader_plan.T

    capacity = (groups * (blocks + 1) + seq_count - 1) // seq_count + 1
    slots = -(-capacity // 16) * 16
    done = {}
    onward = [(i, i + 1) for i in range(seq_count - 1)]

    def while_first(sent):
        return None

    def while_second(sent):
        held = hold(own_tail, sent)
        done["tail"] = lax.ppermute(held, "seq", onward)
        done["low"], done["high"] = select_tails(me.reshape(1), held, plan_cols, inner, outer, slots)

    def while_third(sent):
        done["local"], token = local_part(key_rows, value_rows, taps_rev, response, sent)
        done["block"] = scatter_high(done["low"], done["high"], inner, outer, token)

    def while_fourth(sent):
        done["first"], token, *done["brought"] = carry_part(
            done["local"], done["tail"], taps_rev, query_rows, p1, p2, weight_rows, sent
        )
        done["token"] = token[:1, :1]

    beside = [while_first, while_second, while_third, while_fourth]
    total, incoming, other, last_step = scan_states(own, sent, rates_spread, tokens, inner, beside)
    own_block = done["block"][outer - 1]
    for o, sent_block in enumerate(scatter_outer(done["block"], inner, outer)):
        sent_block = sent_block + done["token"][0, 0].astype(bf16)
        own_block = jnp.where(me // inner == o, sent_block, own_block)
    kept, sent_last = scatter_low(own_block, inner, outer)
    queries, p1_near, p2_near, weights_near = done["brought"]
    gated, energy = gate_part(
        me.reshape(1), last_step, done["first"], done["local"], queries, incoming, other, p1_near, p2_near,
        rates_spread, rate_rows, weights_near,
    )
    mixed, token = norm_part(sum_over_chan(energy), gated, out_gain[None, :])
    handoff = assemble(
        me.reshape(1), last_step, tokens, total, other, rates_spread, norm_spread, plan_cols, kept, sent_last, capacity, token)
    return mixed, handoff


def solution(mesh):
    placed = (
        P("seq", "chan"),
        P("seq", "chan"),
        P("seq", "chan"),
        P("chan", None),
        P("chan", None),
        P("chan", None),
        P("chan"),
        P("chan", None),
    )
    return jax.shard_map(
        per_device,
        mesh=mesh,
        in_specs=placed,
        out_specs=(P("seq", "chan"), P("seq", None, "chan")),
        check_vma=False,
    )
```

```python
import functools
import math

import jax
import jax.numpy as jnp
from jax import lax
from jax.experimental import pallas as pl
from jax.experimental.pallas import tpu as pltpu
from jax.sharding import PartitionSpec as P

D = 8192
GW = 16
MODES = 16
CH = 128
LANES = 128
PER_TILE = LANES // GW
f32 = jnp.float32
bf16 = jnp.bfloat16
highest = lax.Precision.HIGHEST


def params(mib=20):
    return pltpu.CompilerParams(vmem_limit_bytes=mib * 1024 * 1024)


def iota(shape, axis):
    return lax.broadcasted_iota(jnp.int32, shape, axis)


def same_filter(rows, lanes):
    return (iota((rows, lanes), 0) // MODES) == ((iota((rows, lanes), 1) % LANES) // GW)


def tn_dot(a, b, precision=None):
    return lax.dot_general(
        a, b, (((0,), (0,)), ((), ())), preferred_element_type=f32, precision=precision
    )


def by_tile(values):
    groups = values.shape[0]
    copies = (iota((MODES, LANES), 1) % MODES == iota((MODES, LANES), 0)).astype(f32)
    wide = jnp.dot(values, copies, preferred_element_type=f32, precision=highest)
    mine = (iota((groups, LANES), 1) // MODES) == (iota((groups, LANES), 0) % PER_TILE)
    return jnp.where(mine, wide, 0.0).reshape(groups // PER_TILE, PER_TILE, LANES).sum(axis=1)


ANY = pl.BlockSpec(memory_space=pl.ANY)
VMEM = pl.BlockSpec(memory_space=pltpu.VMEM)
HBM = pl.BlockSpec(memory_space=pltpu.HBM)
SMEM = pl.BlockSpec(memory_space=pltpu.SMEM)
TOKEN = jax.ShapeDtypeStruct((8, 128), jnp.float32)


def lanes_at(index, width):
    return pl.ds(pl.multiple_of(index * width, width), width)


def copies(pairs, sems, chunk, width):
    out = []
    for i, (source, target, from_lane, to_lane) in enumerate(pairs):
        out.append(
            pltpu.make_async_copy(
                source.at[:, pl.ds(pl.multiple_of(from_lane + chunk * width, LANES), width)],
                target.at[:, pl.ds(pl.multiple_of(to_lane + chunk * width, LANES), width)],
                sems.at[i, chunk],
            )
        )
    return out


def drain(chunks, width, outputs, out_sems):
    for c in range(chunks):
        for copy in copies(outputs, out_sems, c, width):
            copy.wait()


def product_of(k_ref, v_ref, lanes):
    return (k_ref[:, lanes].astype(f32) * v_ref[:, lanes].astype(f32)).astype(bf16)


def product_kernel(
    chunks, tiles, k_hbm, v_hbm, rates_ref, tail_hbm, p1_hbm, p2_hbm, own_hbm, sent_hbm, rows_ref,
    k_ref, v_ref, tail_ref, p1_ref, p2_ref, own_ref, sent_ref, in_sems, out_sems,
):
    width = tiles * LANES
    inputs = [(k_hbm, k_ref, 0, 0), (v_hbm, v_ref, 0, 0)]
    outputs = [
        (sent_ref, sent_hbm, 0, 0), (own_ref, own_hbm, 0, 0), (tail_ref, tail_hbm, 0, 0),
        (p1_ref, p1_hbm, 0, 0), (p2_ref, p2_hbm, 0, 0),
    ]
    for c in range(chunks):
        for copy in copies(inputs, in_sems, c, width):
            copy.start()
    rows_ref[...] = by_tile(rates_ref[...].T)
    to_end = (CH - iota((CH, LANES), 0)).astype(f32)
    mask = same_filter(LANES, 3 * LANES)
    none = jnp.zeros((CH, LANES), bf16)

    @pl.loop(0, chunks)
    def _(c):
        for copy in copies(inputs, in_sems, c, width):
            copy.wait()
        for t in range(tiles):
            lanes = lanes_at(c * tiles + t, LANES)
            x = product_of(k_ref, v_ref, lanes)
            tail_ref[:, lanes] = x[2 * CH :]
            lam = rows_ref[pl.ds(c * tiles + t, 1), :]
            near = jnp.exp(-to_end * lam)
            decay = jnp.exp(-float(CH) * lam)
            middle = near * decay
            ends = jnp.concatenate([(middle * decay).astype(bf16), middle.astype(bf16), near.astype(bf16)], axis=0)
            x0, x1 = x[:CH], x[CH : 2 * CH]
            wide = jnp.concatenate(
                [x, jnp.concatenate([none, x0, x1], axis=0), jnp.concatenate([none, none, x0], axis=0)], axis=1
            )
            full = tn_dot(ends, wide)
            packed = jnp.where(mask, full, 0.0).reshape(PER_TILE, MODES, 3 * LANES).sum(axis=0)
            own_ref[:, lanes] = packed[:, :LANES]
            sent_ref[:, lanes] = packed[:, :LANES].astype(bf16)
            p2_ref[:, lanes] = packed[:, LANES : 2 * LANES]
            p1_ref[:, lanes] = packed[:, 2 * LANES :]
        for copy in copies(outputs, out_sems, c, width):
            copy.start()

    drain(chunks, width, outputs, out_sems)


def product_and_states(key_rows, value_rows, rates_t):
    tokens, channels = key_rows.shape
    chunks = 4
    tiles = channels // LANES // chunks
    state_shape = jax.ShapeDtypeStruct((MODES, channels), f32)
    return pl.pallas_call(
        functools.partial(product_kernel, chunks, tiles),
        in_specs=[HBM, HBM, VMEM],
        out_specs=[ANY] * 5 + [VMEM],
        out_shape=[
            jax.ShapeDtypeStruct((CH, channels), bf16),
            state_shape, state_shape, state_shape, jax.ShapeDtypeStruct((MODES, channels), bf16),
            jax.ShapeDtypeStruct((channels // LANES, LANES), f32),
        ],
        scratch_shapes=[
            pltpu.VMEM((tokens, channels), bf16), pltpu.VMEM((tokens, channels), bf16), pltpu.VMEM((CH, channels), bf16),
            pltpu.VMEM((MODES, channels), f32), pltpu.VMEM((MODES, channels), f32), pltpu.VMEM((MODES, channels), f32),
            pltpu.VMEM((MODES, channels), bf16),
            pltpu.SemaphoreType.DMA((2, chunks)), pltpu.SemaphoreType.DMA((5, chunks)),
        ],
        compiler_params=params(56),
        cost_estimate=pl.CostEstimate(
            flops=6 * tokens * channels * CH, bytes_accessed=6 * tokens * channels, transcendentals=channels * CH
        ),
        name="product_states",
    )(key_rows, value_rows, rates_t)


FOLD = 4
PARTS = PER_TILE // FOLD


def toeplitz(row):
    return pltpu.roll(jnp.broadcast_to(row, (CH, LANES)), 0, 1, stride=1, stride_axis=0)


def fold_masks():
    group = iota((CH, LANES), 1) // GW
    return [(group % PARTS == a).astype(f32).astype(bf16) for a in range(PARTS)]


def unfold(stacked):
    member = iota((CH, LANES), 1) // GW // PARTS
    out = stacked[:CH]
    for b in range(1, FOLD):
        out = jnp.where(member == b, stacked[b * CH : (b + 1) * CH], out)
    return out


def reversed_lags(taps):
    flip = ((iota((CH, LANES), 0) + iota((CH, LANES), 1)) % CH == 0).astype(f32)
    return jnp.dot(taps, flip, preferred_element_type=f32, precision=highest)


def local_kernel(
    chunks, tiles, k_hbm, v_hbm, taps_rev, response, after,
    out_ref, token_ref, k_ref, v_ref, lhs_all, rhs_all, in_sems,
):
    token_ref[...] = jnp.zeros_like(token_ref)
    half = PARTS * CH
    width = tiles * LANES
    inputs = [(k_hbm, k_ref, 0, 0), (v_hbm, v_ref, 0, 0)]
    for c in range(chunks):
        for copy in copies(inputs, in_sems, c, width):
            copy.start()
    lower = iota((CH, LANES), 1) <= iota((CH, LANES), 0)
    masks = fold_masks()

    @pl.loop(0, chunks)
    def _(c):
        for copy in copies(inputs, in_sems, c, width):
            copy.wait()
        for t in range(tiles):
            lanes = lanes_at(c * tiles + t, LANES)
            lhs_ref, rhs_ref = lhs_all.at[t % 2], rhs_all.at[t % 2]
            x = product_of(k_ref, v_ref, lanes)
            for f in range(PER_TILE):
                a, rows = f % PARTS, slice(f // PARTS * CH, (f // PARTS + 1) * CH)
                row = pl.ds((c * tiles + t) * PER_TILE + f, 1)
                lhs_ref[rows, half + a * CH : half + (a + 1) * CH] = jnp.where(lower, toeplitz(response[row, :]), 0.0).astype(bf16)
                lhs_ref[rows, a * CH : (a + 1) * CH] = jnp.where(lower, 0.0, toeplitz(taps_rev[row, :])).astype(bf16)
            for a in range(PARTS):
                x0, x1, x2 = [x[i * CH : (i + 1) * CH] * masks[a] for i in range(3)]
                rhs_ref[a * CH : (a + 1) * CH, :LANES] = x0
                rhs_ref[a * CH : (a + 1) * CH, LANES:] = x1
                rhs_ref[half + a * CH : half + (a + 1) * CH, :LANES] = x1
                rhs_ref[half + a * CH : half + (a + 1) * CH, LANES:] = x2
            later = jnp.dot(lhs_ref[...], rhs_ref[...], preferred_element_type=f32)
            early = jnp.dot(lhs_ref[:, half:], rhs_ref[:half, :LANES], preferred_element_type=f32)
            out_ref[:CH, lanes] = unfold(early).astype(bf16)
            out_ref[CH : 2 * CH, lanes] = unfold(later[:, :LANES]).astype(bf16)
            out_ref[2 * CH :, lanes] = unfold(later[:, LANES:]).astype(bf16)


def local_part(key_rows, value_rows, taps_rev, response, after):
    tokens, channels = key_rows.shape
    groups = taps_rev.shape[0]
    chunks = 4
    tiles = channels // LANES // chunks
    return pl.pallas_call(
        functools.partial(local_kernel, chunks, tiles),
        in_specs=[ANY, ANY, VMEM, VMEM, ANY],
        out_specs=[VMEM, VMEM],
        out_shape=[jax.ShapeDtypeStruct((tokens, channels), bf16), TOKEN],
        scratch_shapes=[pltpu.VMEM((tokens, channels), bf16)] * 2 + [
            pltpu.VMEM((2, FOLD * CH, 2 * PARTS * CH), bf16), pltpu.VMEM((2, 2 * PARTS * CH, 2 * LANES), bf16),
            pltpu.SemaphoreType.DMA((2, chunks)),
        ],
        compiler_params=params(),
        cost_estimate=pl.CostEstimate(
            flops=groups * CH * 256 * 512 * 2, bytes_accessed=groups * GW * tokens * 4, transcendentals=0
        ),
        name="local_conv",
    )(key_rows, value_rows, taps_rev, response, after)


def carry_kernel(
    chunks, tiles, local_ref, tail_ref, taps_rev, q_hbm, p1_hbm, p2_hbm, weight_hbm, after,
    out_ref, token_ref, q_ref, p1_ref, p2_ref, weight_ref, lhs_all, sems,
):
    bring = [
        pltpu.make_async_copy(source, target, sems.at[i])
        for i, (source, target) in enumerate(
            [(q_hbm, q_ref), (p1_hbm, p1_ref), (p2_hbm, p2_ref), (weight_hbm, weight_ref)]
        )
    ]
    for copy in bring:
        copy.start()
    token_ref[...] = jnp.zeros_like(token_ref)
    lower = iota((CH, LANES), 1) <= iota((CH, LANES), 0)
    masks = fold_masks()

    @pl.loop(0, chunks)
    def _(c):
        for t in range(tiles):
            lanes = lanes_at(c * tiles + t, LANES)
            lhs_ref = lhs_all.at[t % 2]
            for f in range(PER_TILE):
                a, rows = f % PARTS, slice(f // PARTS * CH, (f // PARTS + 1) * CH)
                at = pl.ds((c * tiles + t) * PER_TILE + f, 1)
                lhs_ref[rows, a * CH : (a + 1) * CH] = jnp.where(lower, 0.0, toeplitz(taps_rev[at, :])).astype(bf16)
            tail = tail_ref[:, lanes]
            masked = jnp.concatenate([tail * mask for mask in masks], axis=0)
            carried = unfold(jnp.dot(lhs_ref[...], masked, preferred_element_type=f32))
            out_ref[:, lanes] = (local_ref[:CH, lanes].astype(f32) + carried).astype(bf16)

    for copy in bring:
        copy.wait()


def carry_part(local, tail, taps_rev, query_rows, p1, p2, weight_rows, after):
    tokens, channels = local.shape
    chunks = 4
    tiles = channels // LANES // chunks
    return pl.pallas_call(
        functools.partial(carry_kernel, chunks, tiles),
        in_specs=[VMEM, VMEM, VMEM] + [ANY] * 5,
        out_specs=[VMEM] * 6,
        out_shape=[jax.ShapeDtypeStruct((CH, channels), bf16), TOKEN]
        + [jax.ShapeDtypeStruct(a.shape, a.dtype) for a in (query_rows, p1, p2, weight_rows)],
        scratch_shapes=[pltpu.VMEM((2, FOLD * CH, PARTS * CH), bf16), pltpu.SemaphoreType.DMA((4,))],
        compiler_params=params(),
        cost_estimate=pl.CostEstimate(flops=channels * CH * 1024, bytes_accessed=channels * CH * 6, transcendentals=0),
        name="carry",
    )(local, tail, taps_rev, query_rows, p1, p2, weight_rows, after)


def exact_parts(values):
    high = values.astype(bf16).astype(f32)
    middle = (values - high).astype(bf16).astype(f32)
    return jnp.concatenate([high, middle, values - high - middle], axis=1)


def prepare_kernel(
    rates_ref, factor_ref, residues_ref, taps_ref, spread_ref, norm_ref, taps_rev_ref, response_ref, weight_ref
):
    rates, factor = rates_ref[...].T, factor_ref[...].T
    coeff = residues_ref[...].T * factor
    expand = (iota((PER_TILE, LANES), 1) // GW == iota((PER_TILE, LANES), 0)).astype(f32).astype(bf16)
    for source, target in ((exact_parts(rates), spread_ref), (exact_parts(factor), norm_ref)):
        for t in range(target.shape[1] // LANES):
            wide = tn_dot(source[t * PER_TILE : (t + 1) * PER_TILE].astype(bf16), expand)
            target[:, t * LANES : (t + 1) * LANES] = wide[:MODES] + wide[MODES : 2 * MODES] + wide[2 * MODES :]
    weight_ref[...] = by_tile(coeff)
    lag = ((CH - iota((1, LANES), 1)) % CH).astype(f32)
    sums = reversed_lags(taps_ref[...])
    taps_rev_ref[...] = sums
    for m in range(MODES):
        sums = sums + coeff[:, m : m + 1] * jnp.exp(-rates[:, m : m + 1] * lag)
    response_ref[...] = sums


def prepare(rates_t, factor_t, residues_t, taps):
    groups = taps.shape[0]
    shapes = [(MODES, groups * GW), (MODES, groups * GW), taps.shape, taps.shape, (groups // PER_TILE, LANES)]
    return pl.pallas_call(
        prepare_kernel,
        in_specs=[VMEM] * 4,
        out_specs=[VMEM] * 5,
        out_shape=[jax.ShapeDtypeStruct(shape, f32) for shape in shapes],
        compiler_params=params(),
        name="prepare",
    )(rates_t, factor_t, residues_t, taps)


def cross_of(decays, states):
    mask = same_filter(LANES, len(states) * LANES)
    wide = jnp.concatenate(states, axis=1)
    high = wide.astype(bf16)
    low = wide - high.astype(f32)
    blocks = lambda a: jnp.where(mask, jnp.concatenate([a] * PER_TILE, axis=0), 0.0).astype(bf16)
    stacked = jnp.concatenate([blocks(high.astype(f32)), blocks(low)], axis=0)
    return jnp.dot(jnp.concatenate([decays, decays], axis=1), stacked, preferred_element_type=f32)


def starts_of(lam, weight):
    index = iota((CH, LANES), 0).astype(f32)
    return (weight * jnp.exp(-index * lam)).astype(bf16)


def energy_row(partial):
    return lax.dot_general(
        jnp.ones((8, LANES), f32), partial, (((1,), (1,)), ((), ())), preferred_element_type=f32, precision=highest
    )


def gate_kernel(
    chunks, tiles, step, me_ref, first_ref, local_ref, q_ref, in_ref, other_ref, p1_ref, p2_ref, spread_ref, rates_ref, weight_ref,
    gated_ref, energy_ref, total_ref,
):
    me = me_ref[0]
    offset = ((me & (step - 1)) * gated_ref.shape[0]).astype(f32)
    right = jnp.where((me & step) != 0, 1.0, 0.0)
    total_ref[...] = jnp.zeros_like(total_ref)

    @pl.loop(0, chunks)
    def _(c):
        for t in range(tiles):
            lanes = lanes_at(c * tiles + t, LANES)
            spread = spread_ref[:, lanes]
            decay = jnp.exp(-float(CH) * spread)
            z0 = in_ref[:, lanes] + right * (jnp.exp(-spread * offset) * other_ref[:, lanes].astype(f32))
            entry = decay * z0
            z1 = entry + p1_ref[:, lanes]
            z2 = decay * entry + p2_ref[:, lanes]
            row = pl.ds(c * tiles + t, 1)
            cross = cross_of(starts_of(rates_ref[row, :], weight_ref[row, :]), [z0, z1, z2])
            for i in range(3):
                rows = slice(i * CH, (i + 1) * CH)
                own = first_ref[:, lanes] if i == 0 else local_ref[rows, lanes]
                gated = (own.astype(f32) + cross[:, i * LANES : (i + 1) * LANES]) * q_ref[rows, lanes].astype(f32)
                gated_ref[rows, lanes] = gated.astype(bf16)
                total_ref[rows] += gated * gated

    energy_ref[...] = energy_row(total_ref[...])


def gate_part(me, step, first, local, query_rows, incoming, other, p1, p2, rates_spread, rate_rows, weight_rows):
    tokens, channels = query_rows.shape
    chunks = 4
    tiles = channels // LANES // chunks
    return pl.pallas_call(
        functools.partial(gate_kernel, chunks, tiles, step),
        in_specs=[SMEM] + [VMEM] * 10,
        out_specs=[VMEM, VMEM],
        out_shape=[
            jax.ShapeDtypeStruct((tokens, channels), bf16), jax.ShapeDtypeStruct((8, tokens), f32),
        ],
        scratch_shapes=[pltpu.VMEM((tokens, LANES), f32)],
        compiler_params=params(),
        cost_estimate=pl.CostEstimate(
            flops=channels * CH * 2048, bytes_accessed=channels * tokens * 6, transcendentals=channels * CH
        ),
        name="gate",
    )(me, first, local, query_rows, incoming, other, p1, p2, rates_spread, rate_rows, weight_rows)


def norm_kernel(terms, chunks, tiles, *refs):
    energies, (gated_ref, gain_ref) = refs[:terms], refs[terms : terms + 2]
    out_hbm, token_ref, out_ref, scale_ref, out_sems = refs[-5:]
    token_ref[...] = jnp.zeros_like(token_ref)
    width = tiles * LANES
    rows = gated_ref.shape[0]
    outputs = [(out_ref, out_hbm, 0, 0)]
    energy = sum(ref[...] for ref in energies)
    scale_ref[...] = lax.rsqrt(tn_dot(energy, jnp.full((8, LANES), 0.125, f32), highest) / D + 1e-05)

    @pl.loop(0, chunks)
    def _(c):
        for r in range(0, rows, CH):
            scale = scale_ref[r : r + CH]
            for t in range(tiles):
                lanes = lanes_at(c * tiles + t, LANES)
                value = gated_ref[r : r + CH, lanes].astype(f32) * scale * gain_ref[:, lanes]
                out_ref[r : r + CH, lanes] = value.astype(bf16)
        for copy in copies(outputs, out_sems, c, width):
            copy.start()

    drain(chunks, width, outputs, out_sems)


def norm_part(energies, gated, gain_row):
    rows, channels = gated.shape
    chunks = 4
    tiles = channels // LANES // chunks
    return pl.pallas_call(
        functools.partial(norm_kernel, len(energies), chunks, tiles),
        in_specs=[VMEM] * (len(energies) + 2),
        out_specs=[HBM, VMEM],
        out_shape=[jax.ShapeDtypeStruct((rows, channels), bf16), TOKEN],
        scratch_shapes=[
            pltpu.VMEM((rows, channels), bf16), pltpu.VMEM((rows, LANES), f32), pltpu.SemaphoreType.DMA((1, chunks)),
        ],
        compiler_params=params(),
        cost_estimate=pl.CostEstimate(flops=rows * channels * 2, bytes_accessed=rows * channels * 4, transcendentals=0),
        name="norm",
    )(*energies, gated, gain_row)


def regroup(block):
    shape = block.shape
    sub = iota(shape, 1)
    lane = iota(shape, 2) // GW
    for k in (1, 2, 4):
        up = pltpu.roll(pltpu.roll(block, 8 - k, 1), GW * k, 2)
        down = pltpu.roll(pltpu.roll(block, k, 1), LANES - GW * k, 2)
        row_bit, lane_bit = (sub & k) != 0, (lane & k) != 0
        block = jnp.where(row_bit == lane_bit, block, jnp.where(lane_bit, up, down))
    return block


def ranks_of(present):
    count = present.shape[1]
    before = (iota((count, count), 0) < iota((count, count), 1)).astype(bf16)
    return jnp.dot(present.astype(bf16), before, preferred_element_type=f32)


def select_kernel(blocks, slots, inner, outer, me_ref, tail_hbm, plan_ref, *refs):
    outs, (items_ref, picks_ref, tail_ref, sem) = refs[:2], refs[2:]
    groups = plan_ref.shape[1]

    @pl.when(me_ref[0] != inner * outer - 1)
    def _():
        for out in outs:
            out[...] = jnp.zeros_like(out)

    @pl.when(me_ref[0] == inner * outer - 1)
    def _():
        copy = pltpu.make_async_copy(tail_hbm, tail_ref, sem)
        copy.start()
        copy.wait()
        for g in range(0, groups // PER_TILE, 2):
            halves = []
            for side in range(2):
                tile = g + side
                rows = tail_ref[:, tile * LANES : (tile + 1) * LANES].astype(f32)
                halves.append(regroup(rows.reshape(2 * blocks, 8, LANES)))
            for b in range(blocks):
                for half in range(2):
                    both = jnp.concatenate([halves[0][2 * b + half], halves[1][2 * b + half]], axis=0)
                    items_ref[
                        b * groups + g * 8 : b * groups + (g + 2) * 8, half * LANES : (half + 1) * LANES
                    ] = both.astype(bf16)
        plan = plan_ref[...]
        readers = iota((inner * outer, 1, 1), 0)
        mine = (plan[None] == readers).astype(f32)
        ranks = ranks_of(jnp.sum(mine, axis=1))
        slot = iota((slots, groups), 0).astype(f32).astype(bf16)
        low = inner // 2
        for o in range(outer):
            for p in range(inner):
                r = o * inner + p
                for b in range(blocks):
                    rank = jnp.where(plan[b : b + 1] == r, ranks[r : r + 1], -1.0).astype(bf16)
                    rank = jnp.broadcast_to(rank, (slots, groups))
                    picks_ref[p * slots : (p + 1) * slots, b * groups : (b + 1) * groups] = jnp.where(
                        rank == slot, jnp.ones((), bf16), jnp.zeros((), bf16)
                    )
            total = jnp.dot(picks_ref[...], items_ref[...], preferred_element_type=f32)
            total = total.astype(bf16).reshape(2, low, slots, MODES * GW)
            for side in range(2):
                outs[side][o] = total[side]


def select_tails(me, tail, plan_cols, inner, outer, slots):
    rows = tail.shape[0]
    groups = plan_cols.shape[1]
    blocks = rows // MODES
    vmem = pl.BlockSpec(memory_space=pltpu.VMEM)
    return pl.pallas_call(
        functools.partial(select_kernel, blocks, slots, inner, outer),
        in_specs=[SMEM, ANY, vmem],
        out_specs=[vmem, vmem],
        out_shape=[jax.ShapeDtypeStruct((outer, inner // 2, slots, MODES * GW), bf16)] * 2,
        scratch_shapes=[
            pltpu.VMEM((blocks * groups, MODES * GW), bf16), pltpu.VMEM((inner * slots, blocks * groups), bf16),
            pltpu.VMEM(tail.shape, bf16), pltpu.SemaphoreType.DMA,
        ],
        compiler_params=params(20),
        cost_estimate=pl.CostEstimate(flops=10**9, bytes_accessed=2 * 10**6, transcendentals=0),
        name="select_tails",
    )(me, tail, plan_cols)


def handoff_kernel(step, tokens, me_ref, total_ref, other_ref, spread_ref, norm_ref, plan_ref, kept_ref, sent_ref, after, out_ref, items_ref):
    groups = plan_ref.shape[1]
    capacity = out_ref.shape[2]
    slots = sent_ref.shape[0]
    kept = me_ref[0] % 2 == 1
    plan = plan_ref[...]
    mine = plan == me_ref[0]
    present = jnp.sum(mine.astype(f32), axis=0, keepdims=True)
    rank = ranks_of(jnp.broadcast_to(present, (8, groups)))[:1]
    total, other = total_ref[...], other_ref[...].astype(f32)
    right = (me_ref[0] & step) != 0
    earlier, later = jnp.where(right, other, total), jnp.where(right, total, other)
    final = (jnp.exp(-spread_ref[...] * float(step * tokens)) * earlier + later) * norm_ref[...]
    stack = [
        final[half * 8 : (half + 1) * 8, g * LANES : (g + 1) * LANES]
        for half in range(2) for g in range(groups // PER_TILE)
    ]
    done = regroup(jnp.stack(stack, axis=0)).reshape(2 * groups, LANES).astype(bf16)
    items_ref[:, :LANES] = done[:groups]
    items_ref[:, LANES:] = done[groups:]
    slot = iota((slots, groups), 0).astype(f32)
    last = plan.shape[0] - 1
    at = (jnp.broadcast_to(rank, (slots, groups)) == slot) & mine[last:]
    pick = jnp.where(at, 1.0, 0.0).astype(bf16)
    rows = jnp.dot(pick, items_ref[...], preferred_element_type=f32)
    rows = (rows + jnp.where(kept, kept_ref[...].astype(f32), sent_ref[...].astype(f32))).T
    out_ref[...] = rows[:, :capacity].reshape(out_ref.shape)


def assemble(me, step, tokens, total, other, rates_spread, norm_spread, plan_cols, kept, sent, capacity, after):
    groups = plan_cols.shape[1]
    vmem = pl.BlockSpec(memory_space=pltpu.VMEM)
    out = pl.pallas_call(
        functools.partial(handoff_kernel, step, tokens),
        in_specs=[SMEM] + [vmem] * 7 + [ANY],
        out_specs=vmem,
        out_shape=jax.ShapeDtypeStruct((MODES, GW, capacity), f32),
        scratch_shapes=[pltpu.VMEM((groups, MODES * GW), bf16)],
        compiler_params=params(),
        cost_estimate=pl.CostEstimate(flops=10**9, bytes_accessed=10**6, transcendentals=0),
        name="handoff",
    )(me, total, other, rates_spread, norm_spread, plan_cols, kept, sent, after)
    return out.transpose(2, 0, 1)


def hold_kernel(*refs):
    pass


def hold(array, *after):
    return pl.pallas_call(
        hold_kernel,
        in_specs=[ANY] * (1 + len(after)),
        out_specs=ANY,
        out_shape=jax.ShapeDtypeStruct(array.shape, array.dtype),
        input_output_aliases={0: 0},
        name="hold",
    )(array, *after)


def scatter_high(low, high, inner, outer, token):
    count = inner * outer
    sent = lax.ppermute(low, "seq", [(count - 1, count - 1 - inner // 2)])
    return jnp.where((lax.axis_index("seq") & (inner // 2)) != 0, high, sent + token[0, 0].astype(bf16))


def scatter_outer(block, inner, outer):
    base = inner * (outer - 1)
    heads = (inner // 2 - 1, inner - 1)
    return [
        lax.ppermute(block[o], "seq", [(base + h, o * inner + h) for h in heads]) for o in range(outer - 1)
    ]


def scatter_low(own, inner, outer):
    half = inner // 4
    while True:
        pairs = [(i, i - half) for i in range(inner * outer) if (i + 1) % (2 * half) == 0]
        sent = lax.ppermute(own[:half], "seq", pairs)
        if half == 1:
            return own[1], sent[0]
        own = jnp.where((lax.axis_index("seq") & half) != 0, own[half:], sent)
        half //= 2


def exchange(sent, count, inner, step):
    pairs = [(i, i ^ step) for i in range(count)]
    if step != inner:
        return [lax.ppermute(sent, "seq", pairs)]
    last = lambda i: i % inner == inner - 1
    main = [(i, j) for i, j in pairs if not (last(i) and j > i)]
    extra = [(i - inner // 2, j) for i, j in pairs if last(i) and j > i]
    return [lax.ppermute(sent, "seq", main), lax.ppermute(sent, "seq", extra)]


def scan_states(own, sent, rates_spread, tokens, inner, beside):
    count = lax.axis_size("seq")
    me = lax.axis_index("seq")
    total, incoming = own, jnp.zeros_like(own)
    step = 1
    while True:
        got = exchange(sent, count, inner, step)
        if beside:
            beside.pop(0)(sent)
        if 2 * step >= count:
            return total, incoming, functools.reduce(jnp.add, got), step
        other = sum(part.astype(f32) for part in got)
        right = (me & step) != 0
        offset = ((me & (step - 1)) * tokens).astype(f32)
        decay = jnp.exp(-rates_spread * float(step * tokens))
        total = jnp.where(right, decay * other + total, decay * total + other)
        incoming = jnp.where(right, incoming + jnp.exp(-rates_spread * offset) * other, incoming)
        sent = total.astype(bf16)
        step *= 2


def sum_over_chan(energy):
    if lax.axis_size("chan") == 2:
        return [energy, lax.ppermute(energy, "chan", [(0, 1), (1, 0)])]
    return [lax.psum(energy, "chan")]


def per_device(
    query_rows, key_rows, value_rows, residues, decay_rates, medium_taps, out_gain, reader_plan
):
    tokens, channels = query_rows.shape
    groups, mode_count = residues.shape
    blocks = medium_taps.shape[1] // mode_count
    seq_count = lax.axis_size("seq")
    me = lax.axis_index("seq")

    rates_t = decay_rates.T
    factor_t = jnp.sqrt(-jnp.expm1(-2.0 * rates_t))
    own_tail, p1, p2, own, sent, rate_rows = product_and_states(key_rows, value_rows, rates_t)
    rates_spread, norm_spread, taps_rev, response, weight_rows = prepare(rates_t, factor_t, residues.T, medium_taps)
    inner = 1 << (int(math.log2(seq_count)) // 2)
    outer = seq_count // inner

    plan_cols = reader_plan.T

    capacity = (groups * (blocks + 1) + seq_count - 1) // seq_count + 1
    slots = -(-capacity // 16) * 16
    done = {}
    onward = [(i, i + 1) for i in range(seq_count - 1)]

    def while_first(sent):
        return None

    def while_second(sent):
        held = hold(own_tail, sent)
        done["tail"] = lax.ppermute(held, "seq", onward)
        done["low"], done["high"] = select_tails(me.reshape(1), held, plan_cols, inner, outer, slots)

    def while_third(sent):
        done["local"], token = local_part(key_rows, value_rows, taps_rev, response, sent)
        done["block"] = scatter_high(done["low"], done["high"], inner, outer, token)

    def while_fourth(sent):
        done["first"], token, *done["brought"] = carry_part(
            done["local"], done["tail"], taps_rev, query_rows, p1, p2, weight_rows, sent
        )
        done["token"] = token[:1, :1]

    beside = [while_first, while_second, while_third, while_fourth]
    total, incoming, other, last_step = scan_states(own, sent, rates_spread, tokens, inner, beside)
    own_block = done["block"][outer - 1]
    for o, sent_block in enumerate(scatter_outer(done["block"], inner, outer)):
        sent_block = sent_block + done["token"][0, 0].astype(bf16)
        own_block = jnp.where(me // inner == o, sent_block, own_block)
    kept, sent_last = scatter_low(own_block, inner, outer)
    queries, p1_near, p2_near, weights_near = done["brought"]
    gated, energy = gate_part(
        me.reshape(1), last_step, done["first"], done["local"], queries, incoming, other, p1_near, p2_near,
        rates_spread, rate_rows, weights_near,
    )
    mixed, token = norm_part(sum_over_chan(energy), gated, out_gain[None, :])
    handoff = assemble(
        me.reshape(1), last_step, tokens, total, other, rates_spread, norm_spread, plan_cols, kept, sent_last, capacity, token)
    return mixed, handoff


def solution(mesh):
    placed = (
        P("seq", "chan"),
        P("seq", "chan"),
        P("seq", "chan"),
        P("chan", None),
        P("chan", None),
        P("chan", None),
        P("chan"),
        P("chan", None),
    )
    return jax.shard_map(
        per_device,
        mesh=mesh,
        in_specs=placed,
        out_specs=(P("seq", "chan"), P("seq", None, "chan")),
        check_vma=False,
    )
```

```python
import functools
import math

import jax
import jax.numpy as jnp
from jax import lax
from jax.experimental import pallas as pl
from jax.experimental.pallas import tpu as pltpu
from jax.sharding import PartitionSpec as P

D = 8192
GW = 16
MODES = 16
CH = 128
LANES = 128
PER_TILE = LANES // GW
f32 = jnp.float32
bf16 = jnp.bfloat16
highest = lax.Precision.HIGHEST


def params(mib=20):
    return pltpu.CompilerParams(vmem_limit_bytes=mib * 1024 * 1024)


def iota(shape, axis):
    return lax.broadcasted_iota(jnp.int32, shape, axis)


def same_filter(rows, lanes):
    return (iota((rows, lanes), 0) // MODES) == ((iota((rows, lanes), 1) % LANES) // GW)


def tn_dot(a, b, precision=None):
    return lax.dot_general(
        a, b, (((0,), (0,)), ((), ())), preferred_element_type=f32, precision=precision
    )


def by_tile(values):
    groups = values.shape[0]
    copies = (iota((MODES, LANES), 1) % MODES == iota((MODES, LANES), 0)).astype(f32)
    wide = jnp.dot(values, copies, preferred_element_type=f32, precision=highest)
    mine = (iota((groups, LANES), 1) // MODES) == (iota((groups, LANES), 0) % PER_TILE)
    return jnp.where(mine, wide, 0.0).reshape(groups // PER_TILE, PER_TILE, LANES).sum(axis=1)


ANY = pl.BlockSpec(memory_space=pl.ANY)
VMEM = pl.BlockSpec(memory_space=pltpu.VMEM)
HBM = pl.BlockSpec(memory_space=pltpu.HBM)
SMEM = pl.BlockSpec(memory_space=pltpu.SMEM)
TOKEN = jax.ShapeDtypeStruct((8, 128), jnp.float32)


def lanes_at(index, width):
    return pl.ds(pl.multiple_of(index * width, width), width)


def copies(pairs, sems, chunk, width):
    out = []
    for i, (source, target, from_lane, to_lane) in enumerate(pairs):
        out.append(
            pltpu.make_async_copy(
                source.at[:, pl.ds(pl.multiple_of(from_lane + chunk * width, LANES), width)],
                target.at[:, pl.ds(pl.multiple_of(to_lane + chunk * width, LANES), width)],
                sems.at[i, chunk],
            )
        )
    return out


def drain(chunks, width, outputs, out_sems):
    for c in range(chunks):
        for copy in copies(outputs, out_sems, c, width):
            copy.wait()


def product_of(k_ref, v_ref, lanes):
    return (k_ref[:, lanes].astype(f32) * v_ref[:, lanes].astype(f32)).astype(bf16)


def product_kernel(
    chunks, tiles, k_hbm, v_hbm, rates_ref, tail_hbm, p1_hbm, p2_hbm, own_hbm, sent_hbm, rows_ref,
    k_ref, v_ref, tail_ref, p1_ref, p2_ref, own_ref, sent_ref, in_sems, out_sems,
):
    width = tiles * LANES
    inputs = [(k_hbm, k_ref, 0, 0), (v_hbm, v_ref, 0, 0)]
    outputs = [
        (sent_ref, sent_hbm, 0, 0), (own_ref, own_hbm, 0, 0), (tail_ref, tail_hbm, 0, 0),
        (p1_ref, p1_hbm, 0, 0), (p2_ref, p2_hbm, 0, 0),
    ]
    for c in range(chunks):
        for copy in copies(inputs, in_sems, c, width):
            copy.start()
    rows_ref[...] = by_tile(rates_ref[...].T)
    to_end = (CH - iota((CH, LANES), 0)).astype(f32)
    mask = same_filter(LANES, 3 * LANES)
    none = jnp.zeros((CH, LANES), bf16)

    @pl.loop(0, chunks)
    def _(c):
        for copy in copies(inputs, in_sems, c, width):
            copy.wait()
        for t in range(tiles):
            lanes = lanes_at(c * tiles + t, LANES)
            x = product_of(k_ref, v_ref, lanes)
            tail_ref[:, lanes] = x[2 * CH :]
            lam = rows_ref[pl.ds(c * tiles + t, 1), :]
            near = jnp.exp(-to_end * lam)
            decay = jnp.exp(-float(CH) * lam)
            middle = near * decay
            ends = jnp.concatenate([(middle * decay).astype(bf16), middle.astype(bf16), near.astype(bf16)], axis=0)
            x0, x1 = x[:CH], x[CH : 2 * CH]
            wide = jnp.concatenate(
                [x, jnp.concatenate([none, x0, x1], axis=0), jnp.concatenate([none, none, x0], axis=0)], axis=1
            )
            full = tn_dot(ends, wide)
            packed = jnp.where(mask, full, 0.0).reshape(PER_TILE, MODES, 3 * LANES).sum(axis=0)
            own_ref[:, lanes] = packed[:, :LANES]
            sent_ref[:, lanes] = packed[:, :LANES].astype(bf16)
            p2_ref[:, lanes] = packed[:, LANES : 2 * LANES]
            p1_ref[:, lanes] = packed[:, 2 * LANES :]
        for copy in copies(outputs, out_sems, c, width):
            copy.start()

    drain(chunks, width, outputs, out_sems)


def product_and_states(key_rows, value_rows, rates_t):
    tokens, channels = key_rows.shape
    chunks = 4
    tiles = channels // LANES // chunks
    state_shape = jax.ShapeDtypeStruct((MODES, channels), f32)
    return pl.pallas_call(
        functools.partial(product_kernel, chunks, tiles),
        in_specs=[HBM, HBM, VMEM],
        out_specs=[ANY] * 5 + [VMEM],
        out_shape=[
            jax.ShapeDtypeStruct((CH, channels), bf16),
            state_shape, state_shape, state_shape, jax.ShapeDtypeStruct((MODES, channels), bf16),
            jax.ShapeDtypeStruct((channels // LANES, LANES), f32),
        ],
        scratch_shapes=[
            pltpu.VMEM((tokens, channels), bf16), pltpu.VMEM((tokens, channels), bf16), pltpu.VMEM((CH, channels), bf16),
            pltpu.VMEM((MODES, channels), f32), pltpu.VMEM((MODES, channels), f32), pltpu.VMEM((MODES, channels), f32),
            pltpu.VMEM((MODES, channels), bf16),
            pltpu.SemaphoreType.DMA((2, chunks)), pltpu.SemaphoreType.DMA((5, chunks)),
        ],
        compiler_params=params(56),
        cost_estimate=pl.CostEstimate(
            flops=6 * tokens * channels * CH, bytes_accessed=6 * tokens * channels, transcendentals=channels * CH
        ),
        name="product_states",
    )(key_rows, value_rows, rates_t)


FOLD = 4
PARTS = PER_TILE // FOLD


def toeplitz(row):
    return pltpu.roll(jnp.broadcast_to(row, (CH, LANES)), 0, 1, stride=1, stride_axis=0)


def fold_masks():
    group = iota((CH, LANES), 1) // GW
    return [(group % PARTS == a).astype(f32).astype(bf16) for a in range(PARTS)]


def unfold(stacked):
    member = iota((CH, LANES), 1) // GW // PARTS
    out = stacked[:CH]
    for b in range(1, FOLD):
        out = jnp.where(member == b, stacked[b * CH : (b + 1) * CH], out)
    return out


def reversed_lags(taps):
    flip = ((iota((CH, LANES), 0) + iota((CH, LANES), 1)) % CH == 0).astype(f32)
    return jnp.dot(taps, flip, preferred_element_type=f32, precision=highest)


def local_kernel(
    chunks, tiles, k_hbm, v_hbm, taps_rev, response, after,
    out_ref, token_ref, k_ref, v_ref, lhs_all, rhs_all, in_sems,
):
    token_ref[...] = jnp.zeros_like(token_ref)
    half = PARTS * CH
    width = tiles * LANES
    inputs = [(k_hbm, k_ref, 0, 0), (v_hbm, v_ref, 0, 0)]
    for c in range(chunks):
        for copy in copies(inputs, in_sems, c, width):
            copy.start()
    lower = iota((CH, LANES), 1) <= iota((CH, LANES), 0)
    masks = fold_masks()

    @pl.loop(0, chunks)
    def _(c):
        for copy in copies(inputs, in_sems, c, width):
            copy.wait()
        for t in range(tiles):
            lanes = lanes_at(c * tiles + t, LANES)
            lhs_ref, rhs_ref = lhs_all.at[t % 2], rhs_all.at[t % 2]
            x = product_of(k_ref, v_ref, lanes)
            for f in range(PER_TILE):
                a, rows = f % PARTS, slice(f // PARTS * CH, (f // PARTS + 1) * CH)
                row = pl.ds((c * tiles + t) * PER_TILE + f, 1)
                lhs_ref[rows, half + a * CH : half + (a + 1) * CH] = jnp.where(lower, toeplitz(response[row, :]), 0.0).astype(bf16)
                lhs_ref[rows, a * CH : (a + 1) * CH] = jnp.where(lower, 0.0, toeplitz(taps_rev[row, :])).astype(bf16)
            for a in range(PARTS):
                x0, x1, x2 = [x[i * CH : (i + 1) * CH] * masks[a] for i in range(3)]
                rhs_ref[a * CH : (a + 1) * CH, :LANES] = x0
                rhs_ref[a * CH : (a + 1) * CH, LANES:] = x1
                rhs_ref[half + a * CH : half + (a + 1) * CH, :LANES] = x1
                rhs_ref[half + a * CH : half + (a + 1) * CH, LANES:] = x2
            later = jnp.dot(lhs_ref[...], rhs_ref[...], preferred_element_type=f32)
            early = jnp.dot(lhs_ref[:, half:], rhs_ref[:half, :LANES], preferred_element_type=f32)
            out_ref[:CH, lanes] = unfold(early).astype(bf16)
            out_ref[CH : 2 * CH, lanes] = unfold(later[:, :LANES]).astype(bf16)
            out_ref[2 * CH :, lanes] = unfold(later[:, LANES:]).astype(bf16)


def local_part(key_rows, value_rows, taps_rev, response, after):
    tokens, channels = key_rows.shape
    groups = taps_rev.shape[0]
    chunks = 4
    tiles = channels // LANES // chunks
    return pl.pallas_call(
        functools.partial(local_kernel, chunks, tiles),
        in_specs=[ANY, ANY, VMEM, VMEM, ANY],
        out_specs=[VMEM, VMEM],
        out_shape=[jax.ShapeDtypeStruct((tokens, channels), bf16), TOKEN],
        scratch_shapes=[pltpu.VMEM((tokens, channels), bf16)] * 2 + [
            pltpu.VMEM((2, FOLD * CH, 2 * PARTS * CH), bf16), pltpu.VMEM((2, 2 * PARTS * CH, 2 * LANES), bf16),
            pltpu.SemaphoreType.DMA((2, chunks)),
        ],
        compiler_params=params(),
        cost_estimate=pl.CostEstimate(
            flops=groups * CH * 256 * 512 * 2, bytes_accessed=groups * GW * tokens * 4, transcendentals=0
        ),
        name="local_conv",
    )(key_rows, value_rows, taps_rev, response, after)


def carry_kernel(
    chunks, tiles, local_ref, tail_ref, taps_rev, q_hbm, p1_hbm, p2_hbm, weight_hbm, after,
    out_ref, token_ref, q_ref, p1_ref, p2_ref, weight_ref, lhs_all, sems,
):
    bring = [
        pltpu.make_async_copy(source, target, sems.at[i])
        for i, (source, target) in enumerate(
            [(q_hbm, q_ref), (p1_hbm, p1_ref), (p2_hbm, p2_ref), (weight_hbm, weight_ref)]
        )
    ]
    for copy in bring:
        copy.start()
    token_ref[...] = jnp.zeros_like(token_ref)
    lower = iota((CH, LANES), 1) <= iota((CH, LANES), 0)
    masks = fold_masks()

    @pl.loop(0, chunks)
    def _(c):
        for t in range(tiles):
            lanes = lanes_at(c * tiles + t, LANES)
            lhs_ref = lhs_all.at[t % 2]
            for f in range(PER_TILE):
                a, rows = f % PARTS, slice(f // PARTS * CH, (f // PARTS + 1) * CH)
                at = pl.ds((c * tiles + t) * PER_TILE + f, 1)
                lhs_ref[rows, a * CH : (a + 1) * CH] = jnp.where(lower, 0.0, toeplitz(taps_rev[at, :])).astype(bf16)
            tail = tail_ref[:, lanes]
            masked = jnp.concatenate([tail * mask for mask in masks], axis=0)
            carried = unfold(jnp.dot(lhs_ref[...], masked, preferred_element_type=f32))
            out_ref[:, lanes] = (local_ref[:CH, lanes].astype(f32) + carried).astype(bf16)

    for copy in bring:
        copy.wait()


def carry_part(local, tail, taps_rev, query_rows, p1, p2, weight_rows, after):
    tokens, channels = local.shape
    chunks = 4
    tiles = channels // LANES // chunks
    return pl.pallas_call(
        functools.partial(carry_kernel, chunks, tiles),
        in_specs=[VMEM, VMEM, VMEM] + [ANY] * 5,
        out_specs=[VMEM] * 6,
        out_shape=[jax.ShapeDtypeStruct((CH, channels), bf16), TOKEN]
        + [jax.ShapeDtypeStruct(a.shape, a.dtype) for a in (query_rows, p1, p2, weight_rows)],
        scratch_shapes=[pltpu.VMEM((2, FOLD * CH, PARTS * CH), bf16), pltpu.SemaphoreType.DMA((4,))],
        compiler_params=params(),
        cost_estimate=pl.CostEstimate(flops=channels * CH * 1024, bytes_accessed=channels * CH * 6, transcendentals=0),
        name="carry",
    )(local, tail, taps_rev, query_rows, p1, p2, weight_rows, after)


def exact_parts(values):
    high = values.astype(bf16).astype(f32)
    middle = (values - high).astype(bf16).astype(f32)
    return jnp.concatenate([high, middle, values - high - middle], axis=1)


def prepare_kernel(
    rates_ref, factor_ref, residues_ref, taps_ref, spread_ref, norm_ref, taps_rev_ref, response_ref, weight_ref
):
    rates, factor = rates_ref[...].T, factor_ref[...].T
    coeff = residues_ref[...].T * factor
    expand = (iota((PER_TILE, LANES), 1) // GW == iota((PER_TILE, LANES), 0)).astype(f32).astype(bf16)
    for source, target in ((exact_parts(rates), spread_ref), (exact_parts(factor), norm_ref)):
        for t in range(target.shape[1] // LANES):
            wide = tn_dot(source[t * PER_TILE : (t + 1) * PER_TILE].astype(bf16), expand)
            target[:, t * LANES : (t + 1) * LANES] = wide[:MODES] + wide[MODES : 2 * MODES] + wide[2 * MODES :]
    weight_ref[...] = by_tile(coeff)
    lag = ((CH - iota((1, LANES), 1)) % CH).astype(f32)
    sums = reversed_lags(taps_ref[...])
    taps_rev_ref[...] = sums
    for m in range(MODES):
        sums = sums + coeff[:, m : m + 1] * jnp.exp(-rates[:, m : m + 1] * lag)
    response_ref[...] = sums


def prepare(rates_t, factor_t, residues_t, taps):
    groups = taps.shape[0]
    shapes = [(MODES, groups * GW), (MODES, groups * GW), taps.shape, taps.shape, (groups // PER_TILE, LANES)]
    return pl.pallas_call(
        prepare_kernel,
        in_specs=[VMEM] * 4,
        out_specs=[VMEM] * 5,
        out_shape=[jax.ShapeDtypeStruct(shape, f32) for shape in shapes],
        compiler_params=params(),
        name="prepare",
    )(rates_t, factor_t, residues_t, taps)


def cross_of(decays, states):
    mask = same_filter(LANES, len(states) * LANES)
    wide = jnp.concatenate(states, axis=1)
    high = wide.astype(bf16)
    low = wide - high.astype(f32)
    blocks = lambda a: jnp.where(mask, jnp.concatenate([a] * PER_TILE, axis=0), 0.0).astype(bf16)
    stacked = jnp.concatenate([blocks(high.astype(f32)), blocks(low)], axis=0)
    return jnp.dot(jnp.concatenate([decays, decays], axis=1), stacked, preferred_element_type=f32)


def starts_of(lam, weight):
    index = iota((CH, LANES), 0).astype(f32)
    return (weight * jnp.exp(-index * lam)).astype(bf16)


def energy_row(partial):
    return lax.dot_general(
        jnp.ones((8, LANES), f32), partial, (((1,), (1,)), ((), ())), preferred_element_type=f32, precision=highest
    )


def gate_kernel(
    chunks, tiles, step, me_ref, first_ref, local_ref, q_ref, in_ref, other_ref, p1_ref, p2_ref, spread_ref, rates_ref, weight_ref,
    gated_ref, energy_ref, total_ref,
):
    me = me_ref[0]
    offset = ((me & (step - 1)) * gated_ref.shape[0]).astype(f32)
    right = jnp.where((me & step) != 0, 1.0, 0.0)
    total_ref[...] = jnp.zeros_like(total_ref)

    @pl.loop(0, chunks)
    def _(c):
        for t in range(tiles):
            lanes = lanes_at(c * tiles + t, LANES)
            spread = spread_ref[:, lanes]
            decay = jnp.exp(-float(CH) * spread)
            z0 = in_ref[:, lanes] + right * (jnp.exp(-spread * offset) * other_ref[:, lanes].astype(f32))
            entry = decay * z0
            z1 = entry + p1_ref[:, lanes]
            z2 = decay * entry + p2_ref[:, lanes]
            row = pl.ds(c * tiles + t, 1)
            cross = cross_of(starts_of(rates_ref[row, :], weight_ref[row, :]), [z0, z1, z2])
            for i in range(3):
                rows = slice(i * CH, (i + 1) * CH)
                own = first_ref[:, lanes] if i == 0 else local_ref[rows, lanes]
                gated = (own.astype(f32) + cross[:, i * LANES : (i + 1) * LANES]) * q_ref[rows, lanes].astype(f32)
                gated_ref[rows, lanes] = gated.astype(bf16)
                total_ref[rows] += gated * gated

    energy_ref[...] = energy_row(total_ref[...])


def gate_part(me, step, first, local, query_rows, incoming, other, p1, p2, rates_spread, rate_rows, weight_rows):
    tokens, channels = query_rows.shape
    chunks = 4
    tiles = channels // LANES // chunks
    return pl.pallas_call(
        functools.partial(gate_kernel, chunks, tiles, step),
        in_specs=[SMEM] + [VMEM] * 10,
        out_specs=[VMEM, VMEM],
        out_shape=[
            jax.ShapeDtypeStruct((tokens, channels), bf16), jax.ShapeDtypeStruct((8, tokens), f32),
        ],
        scratch_shapes=[pltpu.VMEM((tokens, LANES), f32)],
        compiler_params=params(),
        cost_estimate=pl.CostEstimate(
            flops=channels * CH * 2048, bytes_accessed=channels * tokens * 6, transcendentals=channels * CH
        ),
        name="gate",
    )(me, first, local, query_rows, incoming, other, p1, p2, rates_spread, rate_rows, weight_rows)


def norm_kernel(terms, chunks, tiles, *refs):
    energies, (gated_ref, gain_ref) = refs[:terms], refs[terms : terms + 2]
    out_hbm, token_ref, out_ref, scale_ref, out_sems = refs[-5:]
    token_ref[...] = jnp.zeros_like(token_ref)
    width = tiles * LANES
    rows = gated_ref.shape[0]
    outputs = [(out_ref, out_hbm, 0, 0)]
    energy = sum(ref[...] for ref in energies)
    scale_ref[...] = lax.rsqrt(tn_dot(energy, jnp.full((8, LANES), 0.125, f32), highest) / D + 1e-05)

    @pl.loop(0, chunks)
    def _(c):
        for r in range(0, rows, CH):
            scale = scale_ref[r : r + CH]
            for t in range(tiles):
                lanes = lanes_at(c * tiles + t, LANES)
                value = gated_ref[r : r + CH, lanes].astype(f32) * scale * gain_ref[:, lanes]
                out_ref[r : r + CH, lanes] = value.astype(bf16)
        for copy in copies(outputs, out_sems, c, width):
            copy.start()

    drain(chunks, width, outputs, out_sems)


def norm_part(energies, gated, gain_row):
    rows, channels = gated.shape
    chunks = 4
    tiles = channels // LANES // chunks
    return pl.pallas_call(
        functools.partial(norm_kernel, len(energies), chunks, tiles),
        in_specs=[VMEM] * (len(energies) + 2),
        out_specs=[HBM, VMEM],
        out_shape=[jax.ShapeDtypeStruct((rows, channels), bf16), TOKEN],
        scratch_shapes=[
            pltpu.VMEM((rows, channels), bf16), pltpu.VMEM((rows, LANES), f32), pltpu.SemaphoreType.DMA((1, chunks)),
        ],
        compiler_params=params(),
        cost_estimate=pl.CostEstimate(flops=rows * channels * 2, bytes_accessed=rows * channels * 4, transcendentals=0),
        name="norm",
    )(*energies, gated, gain_row)


def regroup(block):
    shape = block.shape
    sub = iota(shape, 1)
    lane = iota(shape, 2) // GW
    for k in (1, 2, 4):
        up = pltpu.roll(pltpu.roll(block, 8 - k, 1), GW * k, 2)
        down = pltpu.roll(pltpu.roll(block, k, 1), LANES - GW * k, 2)
        row_bit, lane_bit = (sub & k) != 0, (lane & k) != 0
        block = jnp.where(row_bit == lane_bit, block, jnp.where(lane_bit, up, down))
    return block


def ranks_of(present):
    count = present.shape[1]
    before = (iota((count, count), 0) < iota((count, count), 1)).astype(bf16)
    return jnp.dot(present.astype(bf16), before, preferred_element_type=f32)


def select_kernel(blocks, slots, inner, outer, me_ref, tail_ref, plan_ref, *refs):
    outs, (items_ref, picks_ref) = refs[:2], refs[2:]
    groups = plan_ref.shape[1]

    @pl.when(me_ref[0] != inner * outer - 1)
    def _():
        for out in outs:
            out[...] = jnp.zeros_like(out)

    @pl.when(me_ref[0] == inner * outer - 1)
    def _():
        for g in range(0, groups // PER_TILE, 2):
            halves = []
            for side in range(2):
                tile = g + side
                rows = tail_ref[:, tile * LANES : (tile + 1) * LANES].astype(f32)
                halves.append(regroup(rows.reshape(2 * blocks, 8, LANES)))
            for b in range(blocks):
                for half in range(2):
                    both = jnp.concatenate([halves[0][2 * b + half], halves[1][2 * b + half]], axis=0)
                    items_ref[
                        b * groups + g * 8 : b * groups + (g + 2) * 8, half * LANES : (half + 1) * LANES
                    ] = both.astype(bf16)
        plan = plan_ref[...]
        readers = iota((inner * outer, 1, 1), 0)
        mine = (plan[None] == readers).astype(f32)
        ranks = ranks_of(jnp.sum(mine, axis=1))
        slot = iota((slots, groups), 0).astype(f32).astype(bf16)
        low = inner // 2
        for o in range(outer):
            for p in range(inner):
                r = o * inner + p
                for b in range(blocks):
                    rank = jnp.where(plan[b : b + 1] == r, ranks[r : r + 1], -1.0).astype(bf16)
                    rank = jnp.broadcast_to(rank, (slots, groups))
                    picks_ref[p * slots : (p + 1) * slots, b * groups : (b + 1) * groups] = jnp.where(
                        rank == slot, jnp.ones((), bf16), jnp.zeros((), bf16)
                    )
            total = jnp.dot(picks_ref[...], items_ref[...], preferred_element_type=f32)
            total = total.astype(bf16).reshape(2, low, slots, MODES * GW)
            for side in range(2):
                outs[side][o] = total[side]


def select_tails(me, tail, plan_cols, inner, outer, slots):
    rows = tail.shape[0]
    groups = plan_cols.shape[1]
    blocks = rows // MODES
    vmem = pl.BlockSpec(memory_space=pltpu.VMEM)
    return pl.pallas_call(
        functools.partial(select_kernel, blocks, slots, inner, outer),
        in_specs=[SMEM, vmem, vmem],
        out_specs=[vmem, vmem],
        out_shape=[jax.ShapeDtypeStruct((outer, inner // 2, slots, MODES * GW), bf16)] * 2,
        scratch_shapes=[
            pltpu.VMEM((blocks * groups, MODES * GW), bf16), pltpu.VMEM((inner * slots, blocks * groups), bf16),
        ],
        compiler_params=params(20),
        cost_estimate=pl.CostEstimate(flops=10**9, bytes_accessed=2 * 10**6, transcendentals=0),
        name="select_tails",
    )(me, tail, plan_cols)


def handoff_kernel(step, tokens, me_ref, total_ref, other_ref, spread_ref, norm_ref, plan_ref, kept_ref, sent_ref, after, out_ref, items_ref):
    groups = plan_ref.shape[1]
    capacity = out_ref.shape[2]
    slots = sent_ref.shape[0]
    kept = me_ref[0] % 2 == 1
    plan = plan_ref[...]
    mine = plan == me_ref[0]
    present = jnp.sum(mine.astype(f32), axis=0, keepdims=True)
    rank = ranks_of(jnp.broadcast_to(present, (8, groups)))[:1]
    total, other = total_ref[...], other_ref[...].astype(f32)
    right = (me_ref[0] & step) != 0
    earlier, later = jnp.where(right, other, total), jnp.where(right, total, other)
    final = (jnp.exp(-spread_ref[...] * float(step * tokens)) * earlier + later) * norm_ref[...]
    stack = [
        final[half * 8 : (half + 1) * 8, g * LANES : (g + 1) * LANES]
        for half in range(2) for g in range(groups // PER_TILE)
    ]
    done = regroup(jnp.stack(stack, axis=0)).reshape(2 * groups, LANES).astype(bf16)
    items_ref[:, :LANES] = done[:groups]
    items_ref[:, LANES:] = done[groups:]
    slot = iota((slots, groups), 0).astype(f32)
    last = plan.shape[0] - 1
    at = (jnp.broadcast_to(rank, (slots, groups)) == slot) & mine[last:]
    pick = jnp.where(at, 1.0, 0.0).astype(bf16)
    rows = jnp.dot(pick, items_ref[...], preferred_element_type=f32)
    rows = (rows + jnp.where(kept, kept_ref[...].astype(f32), sent_ref[...].astype(f32))).T
    out_ref[...] = rows[:, :capacity].reshape(out_ref.shape)


def assemble(me, step, tokens, total, other, rates_spread, norm_spread, plan_cols, kept, sent, capacity, after):
    groups = plan_cols.shape[1]
    vmem = pl.BlockSpec(memory_space=pltpu.VMEM)
    out = pl.pallas_call(
        functools.partial(handoff_kernel, step, tokens),
        in_specs=[SMEM] + [vmem] * 7 + [ANY],
        out_specs=vmem,
        out_shape=jax.ShapeDtypeStruct((MODES, GW, capacity), f32),
        scratch_shapes=[pltpu.VMEM((groups, MODES * GW), bf16)],
        compiler_params=params(),
        cost_estimate=pl.CostEstimate(flops=10**9, bytes_accessed=10**6, transcendentals=0),
        name="handoff",
    )(me, total, other, rates_spread, norm_spread, plan_cols, kept, sent, after)
    return out.transpose(2, 0, 1)


def hold_kernel(*refs):
    pass


def hold(array, *after):
    return pl.pallas_call(
        hold_kernel,
        in_specs=[ANY] * (1 + len(after)),
        out_specs=ANY,
        out_shape=jax.ShapeDtypeStruct(array.shape, array.dtype),
        input_output_aliases={0: 0},
        name="hold",
    )(array, *after)


def scatter_high(low, high, inner, outer, token):
    count = inner * outer
    sent = lax.ppermute(low, "seq", [(count - 1, count - 1 - inner // 2)])
    return jnp.where((lax.axis_index("seq") & (inner // 2)) != 0, high, sent + token[0, 0].astype(bf16))


def scatter_outer(block, inner, outer):
    base = inner * (outer - 1)
    heads = (inner // 2 - 1, inner - 1)
    return [
        lax.ppermute(block[o], "seq", [(base + h, o * inner + h) for h in heads]) for o in range(outer - 1)
    ]


def scatter_low(own, inner, outer):
    half = inner // 4
    while True:
        pairs = [(i, i - half) for i in range(inner * outer) if (i + 1) % (2 * half) == 0]
        sent = lax.ppermute(own[:half], "seq", pairs)
        if half == 1:
            return own[1], sent[0]
        own = jnp.where((lax.axis_index("seq") & half) != 0, own[half:], sent)
        half //= 2


def exchange(sent, count, inner, step):
    pairs = [(i, i ^ step) for i in range(count)]
    if step != inner:
        return [lax.ppermute(sent, "seq", pairs)]
    last = lambda i: i % inner == inner - 1
    main = [(i, j) for i, j in pairs if not (last(i) and j > i)]
    extra = [(i - inner // 2, j) for i, j in pairs if last(i) and j > i]
    return [lax.ppermute(sent, "seq", main), lax.ppermute(sent, "seq", extra)]


def scan_states(own, sent, rates_spread, tokens, inner, beside):
    count = lax.axis_size("seq")
    me = lax.axis_index("seq")
    total, incoming = own, jnp.zeros_like(own)
    step = 1
    while True:
        got = exchange(sent, count, inner, step)
        if beside:
            beside.pop(0)(sent)
        if 2 * step >= count:
            return total, incoming, functools.reduce(jnp.add, got), step
        other = sum(part.astype(f32) for part in got)
        right = (me & step) != 0
        offset = ((me & (step - 1)) * tokens).astype(f32)
        decay = jnp.exp(-rates_spread * float(step * tokens))
        total = jnp.where(right, decay * other + total, decay * total + other)
        incoming = jnp.where(right, incoming + jnp.exp(-rates_spread * offset) * other, incoming)
        sent = total.astype(bf16)
        step *= 2


def sum_over_chan(energy):
    if lax.axis_size("chan") == 2:
        return [energy, lax.ppermute(energy, "chan", [(0, 1), (1, 0)])]
    return [lax.psum(energy, "chan")]


def per_device(
    query_rows, key_rows, value_rows, residues, decay_rates, medium_taps, out_gain, reader_plan
):
    tokens, channels = query_rows.shape
    groups, mode_count = residues.shape
    blocks = medium_taps.shape[1] // mode_count
    seq_count = lax.axis_size("seq")
    me = lax.axis_index("seq")

    rates_t = decay_rates.T
    factor_t = jnp.sqrt(-jnp.expm1(-2.0 * rates_t))
    own_tail, p1, p2, own, sent, rate_rows = product_and_states(key_rows, value_rows, rates_t)
    rates_spread, norm_spread, taps_rev, response, weight_rows = prepare(rates_t, factor_t, residues.T, medium_taps)
    inner = 1 << (int(math.log2(seq_count)) // 2)
    outer = seq_count // inner

    plan_cols = reader_plan.T

    capacity = (groups * (blocks + 1) + seq_count - 1) // seq_count + 1
    slots = -(-capacity // 16) * 16
    done = {}
    onward = [(i, i + 1) for i in range(seq_count - 1)]

    def while_first(sent):
        return None

    def while_second(sent):
        held = hold(own_tail, sent)
        done["tail"] = lax.ppermute(held, "seq", onward)
        done["low"], done["high"] = select_tails(me.reshape(1), held, plan_cols, inner, outer, slots)

    def while_third(sent):
        done["local"], token = local_part(key_rows, value_rows, taps_rev, response, sent)
        done["block"] = scatter_high(done["low"], done["high"], inner, outer, token)

    def while_fourth(sent):
        done["first"], token, *done["brought"] = carry_part(
            done["local"], done["tail"], taps_rev, query_rows, p1, p2, weight_rows, sent
        )
        done["token"] = token[:1, :1]

    beside = [while_first, while_second, while_third, while_fourth]
    total, incoming, other, last_step = scan_states(own, sent, rates_spread, tokens, inner, beside)
    own_block = done["block"][outer - 1]
    for o, sent_block in enumerate(scatter_outer(done["block"], inner, outer)):
        sent_block = sent_block + done["token"][0, 0].astype(bf16)
        own_block = jnp.where(me // inner == o, sent_block, own_block)
    kept, sent_last = scatter_low(own_block, inner, outer)
    queries, p1_near, p2_near, weights_near = done["brought"]
    gated, energy = gate_part(
        me.reshape(1), last_step, done["first"], done["local"], queries, incoming, other, p1_near, p2_near,
        rates_spread, rate_rows, weights_near,
    )
    mixed, token = norm_part(sum_over_chan(energy), gated, out_gain[None, :])
    handoff = assemble(
        me.reshape(1), last_step, tokens, total, other, rates_spread, norm_spread, plan_cols, kept, sent_last, capacity, token)
    return mixed, handoff


def solution(mesh):
    placed = (
        P("seq", "chan"),
        P("seq", "chan"),
        P("seq", "chan"),
        P("chan", None),
        P("chan", None),
        P("chan", None),
        P("chan"),
        P("chan", None),
    )
    return jax.shard_map(
        per_device,
        mesh=mesh,
        in_specs=placed,
        out_specs=(P("seq", "chan"), P("seq", None, "chan")),
        check_vma=False,
    )
```
